128 devices in a mesh: chan: 16 (over z, y_lo, core), tm: 8 (over x, y_hi).
Axes of the slice: x: 4, y: 4 (y_hi: 2, y_lo: 2; y = y_hi * 2 + y_lo), z: 4, core: 2. Of those that a mesh axis runs over, the one named last changes fastest.
Arguments:
- traces: bfloat16 [2048, 256, 512], P('chan', 'tm'), may hold values from -34 to 34
- pairing: int32 [3, 16], replicated, may hold values from 0 to 15, as said below
Outputs:
- correlations: float32 [3, 64, 2048, 128], P(None, 'tm', 'chan')
The draws below stay inside these ranges and needn't reach their ends.
Inputs may be any that keep to these rules, and one draw needn't show every extreme that they name: Each row pairs every block with another block, both ways (pairing[r, pairing[r, c]] = c, never c itself); the rows are distinct rounds of one round-robin tournament, so no two blocks meet twice.
All inputs are finite; a program needn't handle non-finite values.
Results may differ from the reference program's by a relative error of at most 0.0068.
Values may be sent and summed in bfloat16 or wider, within the bound.
No kernel may reach another device: no remote copies, remote signals or barrier semaphores. Data moves between devices by JAX's collectives and lax.ppermute only.
A program may use at most 128 MiB of HBM per device.

```python
import math
import jax
import jax.numpy as jnp
from jax import lax

CH_DEV = 128
FREQS = 256
LAGS = 64
W_DEV = 32
ROUNDS = 3
SAMPLES = 512
CHANNELS = 2048
WINDOWS = 256
N_CHAN = 16
N_TM = 8


def draw_pairing(key, part):
    key = jax.random.fold_in(key, 7)
    key_one, key_two = jax.random.split(key)
    relabel = jax.random.permutation(key_one, N_CHAN).astype(jnp.int32)
    chosen = jax.random.permutation(key_two, N_CHAN - 1).astype(jnp.int32)[:ROUNDS]
    player = jnp.arange(N_CHAN, dtype=jnp.int32)[None, :]
    last_one = N_CHAN - 1
    other = (2 * chosen[:, None] - player) % last_one
    other = jnp.where(other == player, last_one, other)
    other = jnp.where(player == last_one, chosen[:, None], other)
    table = jnp.zeros((ROUNDS, N_CHAN), jnp.int32)
    table = table.at[:, relabel].set(relabel[other])
    return table


def draw_traces(key, part):
    key = jax.random.fold_in(key, 11)
    keys = jax.random.split(key, 4)
    shape = (CHANNELS, WINDOWS, SAMPLES + 2)
    noise = jnp.clip(jax.random.normal(keys[0], shape, jnp.float32), -4.0, 4.0)
    first_sensor = jax.random.uniform(keys[1], (CHANNELS, 1, 1), jnp.float32, -0.9, 0.9)
    second_sensor = jax.random.uniform(keys[2], (CHANNELS, 1, 1), jnp.float32, -0.9, 0.9)
    level = jnp.exp(jax.random.uniform(keys[3], (CHANNELS, WINDOWS, 1), jnp.float32, math.log(0.3), math.log(3.0)))
    noise_signal = level * (noise[:, :, 2:] + first_sensor * noise[:, :, 1:-1] + second_sensor * noise[:, :, :-2])
    return noise_signal.astype(jnp.bfloat16)


def setup_inputs(seed: int = 0) -> dict:
    arg_keys = jax.random.split(jax.random.key(seed), 3)
    traces = draw_traces(jax.random.fold_in(arg_keys[2], 71), 0)
    pairing = draw_pairing(jax.random.fold_in(arg_keys[2], 71), 0)
    return dict(traces=traces, pairing=pairing)


WATER = 1.0
EPS = 1e-06

def forward_table(num_freqs, samples):
    freq_idx = jnp.arange(num_freqs, dtype=jnp.int32)[:, None]
    sample_idx = jnp.arange(samples, dtype=jnp.int32)[None, :]
    phase_angles = (freq_idx * sample_idx % samples).astype(jnp.float32) * (2.0 * math.pi / samples)
    return jnp.concatenate([jnp.cos(phase_angles), -jnp.sin(phase_angles)], 0).astype(jnp.bfloat16)

def lag_table(num_lags, num_freqs, samples):
    lag_idx = jnp.arange(num_lags, dtype=jnp.int32)[:, None]
    freq_idx = jnp.arange(num_freqs, dtype=jnp.int32)[None, :]
    phase_angles = (lag_idx * freq_idx % samples).astype(jnp.float32) * (2.0 * math.pi / samples)
    return jnp.concatenate([jnp.cos(phase_angles), -jnp.sin(phase_angles)], 1).astype(jnp.bfloat16)

def taper_window(samples):
    sample_pos = jnp.arange(samples, dtype=jnp.float32)
    return 0.5 - 0.5 * jnp.cos((sample_pos + 0.5) * (2.0 * math.pi / samples))

def whitened(block_traces):
    samples = block_traces.shape[2]
    num_freqs = samples // 2
    waveform = block_traces.astype(jnp.float32)
    waveform = waveform - lax.optimization_barrier(jnp.mean(waveform, axis=2, keepdims=True))
    tapered = lax.optimization_barrier((waveform * taper_window(samples)).astype(jnp.bfloat16))
    spectra = jnp.einsum('cws,ks->kwc', tapered.astype(jnp.float32), forward_table(num_freqs, samples).astype(jnp.float32))
    spectra = spectra.reshape(2, num_freqs, block_traces.shape[1], block_traces.shape[0])
    power_spec = spectra[0] * spectra[0] + spectra[1] * spectra[1]
    level_mean = lax.optimization_barrier(jnp.mean(power_spec, axis=0))
    return (spectra * lax.rsqrt(power_spec + WATER * level_mean + EPS)).astype(jnp.bfloat16)

def stacked_rows(spec):
    return jnp.stack([jnp.concatenate([spec[0], spec[1]], 1), jnp.concatenate([spec[1], -spec[0]], 1)])

def reference(traces, pairing):
    lag_weights = lag_table(LAGS, FREQS, SAMPLES).astype(jnp.float32)
    block_traces = traces.reshape(N_CHAN, CH_DEV, WINDOWS, SAMPLES)
    spectra_all = lax.map(whitened, block_traces)
    norm_scale = 1.0 / math.sqrt(FREQS * WINDOWS)

    def pair_lags(indices):
        own_index, partner_index = indices
        own_spec = lax.dynamic_index_in_dim(spectra_all, own_index, 0, keepdims=False)
        partner_spec = lax.dynamic_index_in_dim(spectra_all, partner_index, 0, keepdims=False)

        def group_sum(total, group_idx):
            first = (group_idx * W_DEV).astype(jnp.int32)
            own_part = lax.dynamic_slice_in_dim(own_spec, first, W_DEV, 2)
            partner_part = lax.dynamic_slice_in_dim(partner_spec, first, W_DEV, 2)
            own_rows = stacked_rows(own_part)
            partner_rows = jnp.concatenate([partner_part[0], partner_part[1]], 1)
            cross_spectrum = jnp.einsum('rfki,fkj->rfij', own_rows.astype(jnp.float32), partner_rows.astype(jnp.float32)).astype(jnp.bfloat16)
            cross_spectrum = lax.optimization_barrier(cross_spectrum)
            return (total + cross_spectrum.astype(jnp.float32), None)
        total, _ = lax.scan(group_sum, jnp.zeros((2, FREQS, CH_DEV, CH_DEV), jnp.float32), jnp.arange(N_TM, dtype=jnp.int32))
        lagged = jnp.dot(lag_weights, total.reshape(2 * FREQS, CH_DEV * CH_DEV), precision=lax.Precision.HIGHEST)
        return lagged.reshape(LAGS, CH_DEV, CH_DEV) * norm_scale
    rounds_out = []
    for round_idx in range(ROUNDS):
        per_block = lax.map(pair_lags, (jnp.arange(N_CHAN, dtype=jnp.int32), pairing[round_idx].astype(jnp.int32)))
        rounds_out.append(jnp.transpose(per_block, (1, 0, 2, 3)).reshape(LAGS, CHANNELS, CH_DEV))
    return jnp.stack(rounds_out)
```

```python
import functools
import math

import jax
import jax.numpy as jnp
import numpy as np
from jax import lax
from jax.experimental import pallas as pl
from jax.experimental.pallas import tpu as pltpu
from jax.sharding import PartitionSpec as P

FREQS = 256
SAMPLES = 512
LAGS = 64
CH = 128
WIN = 32
GROUPS = 64
ROWS = 256
N_CHAN = 16
N_TM = 8
WATER = 1.0
EPS = 1e-06
F32 = jnp.float32
BF16 = jnp.bfloat16


def forward_rows():
    freq = jnp.arange(FREQS, dtype=jnp.int32)[:, None]
    sample = jnp.arange(SAMPLES, dtype=jnp.int32)[None, :]
    phase = (freq * sample % SAMPLES).astype(F32) * (2.0 * math.pi / SAMPLES)
    both = jnp.stack([jnp.cos(phase), -jnp.sin(phase)], 0)
    both = both.reshape(2, GROUPS, 4, SAMPLES).transpose(1, 0, 2, 3)
    return both.reshape(2 * FREQS, SAMPLES).astype(BF16)


def lag_rows():
    lag = jnp.arange(LAGS, dtype=jnp.int32)[:, None]
    freq = jnp.arange(FREQS, dtype=jnp.int32)[None, :]
    phase = (lag * freq % SAMPLES).astype(F32) * (2.0 * math.pi / SAMPLES)
    both = jnp.stack([jnp.cos(phase), -jnp.sin(phase)], 0)
    both = both.reshape(2, N_TM, 1, 8, GROUPS, 1, 4)
    parity = jnp.eye(2, dtype=F32).reshape(1, 1, 2, 1, 1, 2, 1)
    return (both * parity).reshape(2, 2 * LAGS, 2 * FREQS).astype(BF16)


def taper_row():
    pos = jnp.arange(SAMPLES, dtype=F32)
    return (0.5 - 0.5 * jnp.cos((pos + 0.5) * (2.0 * math.pi / SAMPLES))).reshape(1, SAMPLES)


def whiten_kernel(traces, taper, table, out, tapered):
    def taper_step(step, carry):
        rows = traces[pl.ds(step * 8, 8)].astype(F32)
        rows = rows - jnp.mean(rows, axis=2, keepdims=True)
        rows = (rows * taper[...].reshape(1, 1, SAMPLES)).reshape(8 * WIN, SAMPLES)
        for tile in range(4):
            tapered[tile, pl.ds(step * 8 * WIN, 8 * WIN), :] = rows[:, tile * 128 : tile * 128 + 128]
        return carry

    lax.fori_loop(0, CH // 8, taper_step, 0)

    def window_pair(pair, carry):
        parts = []
        for half in range(2):
            tiles = [
                tapered[tile, pl.ds(pair * 2 + half, CH, stride=WIN), :] for tile in range(4)
            ]
            parts.append(jnp.concatenate(tiles, axis=1).astype(BF16))
        columns = jnp.concatenate(parts, axis=0)
        spec = lax.dot_general(
            table[...], columns, (((1,), (1,)), ((), ())), preferred_element_type=F32
        ).reshape(GROUPS, 8, 2 * CH)
        square = spec * spec
        level = jnp.sum(jnp.sum(square, axis=0), axis=0, keepdims=True) * (1.0 / FREQS)
        power = square + pltpu.roll(square, 4, 1)
        white = spec * lax.rsqrt(power + WATER * level.reshape(1, 1, 2 * CH) + EPS)
        white = jnp.concatenate([white[:, :, :CH], white[:, :, CH:]], axis=1)
        out[:, pl.ds(pl.multiple_of(pair * 16, 16), 16), :] = white.astype(BF16)
        return carry

    lax.fori_loop(0, WIN // 2, window_pair, 0)


def whiten(traces):
    return pl.pallas_call(
        whiten_kernel,
        out_shape=jax.ShapeDtypeStruct((GROUPS, ROWS, CH), BF16),
        in_specs=[pl.BlockSpec(memory_space=pltpu.VMEM)] * 3,
        out_specs=pl.BlockSpec(memory_space=pltpu.VMEM),
        scratch_shapes=[pltpu.VMEM((4, CH * WIN, 128), F32)],
        compiler_params=pltpu.CompilerParams(vmem_limit_bytes=40 * 2**20),
        cost_estimate=pl.CostEstimate(flops=2 * 2**30, bytes_accessed=2**23, transcendentals=2**20),
        name="whiten",
    )(traces, taper_row(), forward_rows())


def expand_kernel(spec, out, wide):
    lane = lax.broadcasted_iota(jnp.int32, (CH, ROWS), 1)
    for part in range(spec.shape[0]):
        turned = spec[part].astype(F32).T
        for f in range(4):
            kept = jnp.where(lane % 4 == f, turned, 0.0)
            for tile in range(2):
                wide[tile, pl.ds(f, CH, stride=4), :] = kept[:, tile * 128 : tile * 128 + 128]
        for tile in range(2):
            out[part, :, tile * 128 : tile * 128 + 128] = wide[tile].astype(BF16)


def expand(spec):
    per = 4
    return pl.pallas_call(
        expand_kernel,
        grid=(GROUPS // per,),
        out_shape=jax.ShapeDtypeStruct((GROUPS, 4 * CH, ROWS), BF16),
        in_specs=[pl.BlockSpec((per, ROWS, CH), lambda g: (g, 0, 0))],
        out_specs=pl.BlockSpec((per, 4 * CH, ROWS), lambda g: (g, 0, 0)),
        scratch_shapes=[pltpu.VMEM((2, 4 * CH, 128), F32)],
        compiler_params=pltpu.CompilerParams(vmem_limit_bytes=32 * 2**20),
        cost_estimate=pl.CostEstimate(flops=2**26, bytes_accessed=20 * 2**20, transcendentals=0),
        name="expand",
    )(spec)


def correlate_kernel(both_signs, steps, own, partner, table, out, cross):
    step = pl.program_id(0)
    per = own.shape[0]
    sub = lax.broadcasted_iota(jnp.int32, (WIN, 8, CH), 1)
    for pair in range(per // 2):
        halves = []
        for half in range(2):
            part = partner[2 * pair + half]
            wide = part.astype(F32).reshape(WIN, 8, CH)
            turned = jnp.where(sub < 4, -1.0, 1.0) * pltpu.roll(wide, 4, 1)
            right = jnp.concatenate([part, turned.reshape(ROWS, CH).astype(BF16)], axis=1)
            prod = jnp.dot(own[2 * pair + half], right, preferred_element_type=F32)
            halves.append(prod.reshape(CH // 2, 8, 2 * CH))
        rows = jnp.concatenate(halves, axis=1).astype(BF16)
        first = pl.multiple_of((step * (per // 2) + pair) * 16, 16)
        cross[:, pl.ds(first, 16), :] = rows

    @pl.when(step == steps - 1)
    def _():
        scale = 1.0 / math.sqrt(FREQS * WIN * N_TM)

        def channel_pairs(idx, carry):
            first, second = cross[2 * idx], cross[2 * idx + 1]
            even = jnp.concatenate([first[:, :CH], second[:, :CH]], axis=1)
            odd = jnp.concatenate([first[:, CH:], second[:, CH:]], axis=1)
            even = jnp.dot(table[0], even, preferred_element_type=F32)
            odd = jnp.dot(table[1], odd, preferred_element_type=F32)
            signed = [(even + odd) * scale]
            if both_signs:
                signed.append((even - odd) * scale)
            for sign, value in enumerate(signed):
                value = value.astype(BF16).reshape(N_TM, 16, 2 * CH)
                out[:, sign, 2 * idx] = value[:, :, :CH]
                out[:, sign, 2 * idx + 1] = value[:, :, CH:]
            return carry

        lax.fori_loop(0, CH // 4, channel_pairs, 0)


def correlate(own, partner, both_signs):
    per = 4
    steps = GROUPS // per
    signs = 2 if both_signs else 1
    return pl.pallas_call(
        functools.partial(correlate_kernel, both_signs, steps),
        grid=(steps,),
        out_shape=jax.ShapeDtypeStruct((N_TM, signs, CH // 2, 16, CH), BF16),
        in_specs=[
            pl.BlockSpec((per, 4 * CH, ROWS), lambda g: (g, 0, 0)),
            pl.BlockSpec((per, ROWS, CH), lambda g: (g, 0, 0)),
            pl.BlockSpec((2, 2 * LAGS, 2 * FREQS), lambda g: (0, 0, 0)),
        ],
        out_specs=pl.BlockSpec((N_TM, signs, CH // 2, 16, CH), lambda g: (0, 0, 0, 0, 0)),
        scratch_shapes=[pltpu.VMEM((CH // 2, 2 * FREQS, 2 * CH), BF16)],
        compiler_params=pltpu.CompilerParams(vmem_limit_bytes=48 * 2**20),
        cost_estimate=pl.CostEstimate(flops=2**34, bytes_accessed=24 * 2**20, transcendentals=0),
        name="correlate_both" if both_signs else "correlate_one",
    )(own, partner, lag_rows())


def pick_kernel(index, source, out):
    out[...] = source[...]


def pick(source, index):
    block = (1,) + source.shape[1:]
    zeros = (0,) * (source.ndim - 1)
    return pl.pallas_call(
        pick_kernel,
        grid_spec=pltpu.PrefetchScalarGridSpec(
            num_scalar_prefetch=1,
            grid=(source.shape[0],),
            in_specs=[pl.BlockSpec(block, lambda c, index: (index[c],) + zeros)],
            out_specs=pl.BlockSpec(block, lambda c, index: (c,) + zeros),
        ),
        out_shape=jax.ShapeDtypeStruct(source.shape, source.dtype),
        cost_estimate=pl.CostEstimate(
            flops=0, bytes_accessed=2 * source.size * source.dtype.itemsize, transcendentals=0
        ),
        name="pick",
    )(index, source)


def at(values, index):
    hit = index[:, None] == jnp.arange(N_CHAN, dtype=jnp.int32)[None, :]
    return jnp.sum(jnp.where(hit, values[None, :], 0), axis=1)


def orient(pairing):
    zero, one = pairing[0], pairing[1]
    hop = at(one, zero)
    least = jnp.arange(N_CHAN, dtype=jnp.int32)
    for _ in range(3):
        least = jnp.minimum(least, at(least, hop))
        hop = at(hop, hop)
    handles_zero = least < at(least, zero)
    return handles_zero, jnp.where(handles_zero, zero, one), jnp.where(handles_zero, one, zero)


def over_chan(blocks):
    return lax.all_to_all(blocks, "chan", split_axis=0, concat_axis=0, tiled=True)


def sum_over_tm(parts):
    me = lax.axis_index("tm")
    mine_x, mine_y = me // 2, me % 2
    shape = parts.shape[1:]
    parts = parts.reshape((4, 2) + shape)
    total = lax.dynamic_index_in_dim(parts, mine_x, 0, keepdims=False).astype(F32)
    got = []
    for shift in (2, 1, 3):
        block = lax.dynamic_index_in_dim(parts, (mine_x + shift) % 4, 0, keepdims=False)
        route = [(x * 2 + y, (x + shift) % 4 * 2 + y) for x in range(4) for y in range(2)]
        got.append(lax.ppermute(block, "tm", route))
    for block in got:
        total = total + block.astype(F32)
    other = lax.dynamic_index_in_dim(total, 1 - mine_y, 0, keepdims=False).astype(BF16)
    other = lax.ppermute(other, "tm", [(t, t ^ 1) for t in range(N_TM)])
    return lax.dynamic_index_in_dim(total, mine_y, 0, keepdims=False) + other.astype(F32)


def body(traces, pairing):
    spec = whiten(traces)
    spread = over_chan(spec.reshape(N_CHAN, GROUPS // N_CHAN * ROWS, CH))
    own = expand(spec)
    handles_zero, handled, other = orient(pairing)
    first = over_chan(pick(spread, handled)).reshape(GROUPS, ROWS, CH)
    second = over_chan(pick(spread, pairing[2])).reshape(GROUPS, ROWS, CH)
    pair_sum = sum_over_tm(correlate(own, first, True))
    last_sum = sum_over_tm(correlate(own, second, False))

    def lags_first(value):
        return value.reshape(CH, 8, CH).transpose(1, 0, 2)

    forward = lags_first(pair_sum[0])
    backward = pair_sum[1].reshape(N_CHAN, 64, CH).astype(BF16)
    backward = over_chan(pick(over_chan(backward), other))
    backward = backward.astype(F32).reshape(CH, 8, CH).transpose(1, 2, 0)
    mine = lax.dynamic_index_in_dim(handles_zero, lax.axis_index("chan"), 0, keepdims=False)
    return jnp.stack(
        [
            jnp.where(mine, forward, backward),
            jnp.where(mine, backward, forward),
            lags_first(last_sum[0]),
        ]
    )


def solution(mesh):
    return jax.shard_map(
        body,
        mesh=mesh,
        in_specs=(P("chan", "tm", None), P()),
        out_specs=P(None, "tm", "chan", None),
        check_vma=False,
    )
```

```python
import functools
import math

import jax
import jax.numpy as jnp
import numpy as np
from jax import lax
from jax.experimental import pallas as pl
from jax.experimental.pallas import tpu as pltpu
from jax.sharding import PartitionSpec as P

FREQS = 256
SAMPLES = 512
LAGS = 64
CH = 128
WIN = 32
GROUPS = 64
ROWS = 256
N_CHAN = 16
N_TM = 8
WATER = 1.0
EPS = 1e-06
F32 = jnp.float32
BF16 = jnp.bfloat16


def forward_rows():
    freq = np.arange(FREQS)[:, None]
    sample = np.arange(SAMPLES)[None, :]
    phase = (freq * sample % SAMPLES) * (2.0 * math.pi / SAMPLES)
    both = np.stack([np.cos(phase), -np.sin(phase)], 0)
    both = both.reshape(2, GROUPS, 4, SAMPLES).transpose(1, 0, 2, 3)
    return both.reshape(2 * FREQS, SAMPLES).astype(np.float32).astype(BF16)


def lag_rows():
    lag = np.arange(LAGS)[:, None]
    freq = np.arange(FREQS)[None, :]
    phase = (lag * freq % SAMPLES) * (2.0 * math.pi / SAMPLES)
    both = np.stack([np.cos(phase), -np.sin(phase)], 0)
    both = both.reshape(2, N_TM, 1, 8, GROUPS, 1, 4)
    parity = np.eye(2).reshape(1, 1, 2, 1, 1, 2, 1)
    return (both * parity).reshape(2, 2 * LAGS, 2 * FREQS).astype(np.float32).astype(BF16)


def taper_row():
    pos = np.arange(SAMPLES)
    taper = 0.5 - 0.5 * np.cos((pos + 0.5) * (2.0 * math.pi / SAMPLES))
    return taper.astype(np.float32).reshape(1, SAMPLES)


def whiten_kernel(traces, taper, table, out, tapered):
    def taper_step(step, carry):
        rows = traces[pl.ds(step * 8, 8)].astype(F32)
        rows = rows - jnp.mean(rows, axis=2, keepdims=True)
        rows = (rows * taper[...].reshape(1, 1, SAMPLES)).reshape(8 * WIN, SAMPLES)
        for tile in range(4):
            tapered[tile, pl.ds(step * 8 * WIN, 8 * WIN), :] = rows[:, tile * 128 : tile * 128 + 128]
        return carry

    lax.fori_loop(0, CH // 8, taper_step, 0, unroll=2)

    def window_pair(pair, carry):
        parts = []
        for half in range(2):
            tiles = [
                tapered[tile, pl.ds(pair * 2 + half, CH, stride=WIN), :] for tile in range(4)
            ]
            parts.append(jnp.concatenate(tiles, axis=1).astype(BF16))
        columns = jnp.concatenate(parts, axis=0)
        spec = lax.dot_general(
            table[...], columns, (((1,), (1,)), ((), ())), preferred_element_type=F32
        ).reshape(GROUPS, 8, 2 * CH)
        square = spec * spec
        level = jnp.sum(jnp.sum(square, axis=0), axis=0, keepdims=True) * (1.0 / FREQS)
        power = square + pltpu.roll(square, 4, 1)
        white = spec * lax.rsqrt(power + WATER * level.reshape(1, 1, 2 * CH) + EPS)
        white = jnp.concatenate([white[:, :, :CH], white[:, :, CH:]], axis=1)
        out[:, pl.ds(pl.multiple_of(pair * 16, 16), 16), :] = white.astype(BF16)
        return carry

    lax.fori_loop(0, WIN // 2, window_pair, 0, unroll=4)


def whiten(traces):
    return pl.pallas_call(
        whiten_kernel,
        out_shape=jax.ShapeDtypeStruct((GROUPS, ROWS, CH), BF16),
        in_specs=[pl.BlockSpec(memory_space=pltpu.VMEM)] * 3,
        out_specs=pl.BlockSpec(memory_space=pltpu.VMEM),
        scratch_shapes=[pltpu.VMEM((4, CH * WIN, 128), F32)],
        compiler_params=pltpu.CompilerParams(vmem_limit_bytes=40 * 2**20),
        cost_estimate=pl.CostEstimate(flops=2 * 2**30, bytes_accessed=2**23, transcendentals=2**20),
        name="whiten",
    )(traces, jnp.asarray(taper_row()), jnp.asarray(forward_rows()))


def expand_kernel(spec, out, wide):
    lane = lax.broadcasted_iota(jnp.int32, (CH, ROWS), 1)
    for part in range(spec.shape[0]):
        turned = spec[part].astype(F32).T
        for f in range(4):
            kept = jnp.where(lane % 4 == f, turned, 0.0)
            for tile in range(2):
                wide[tile, pl.ds(f, CH, stride=4), :] = kept[:, tile * 128 : tile * 128 + 128]
        for tile in range(2):
            out[part, :, tile * 128 : tile * 128 + 128] = wide[tile].astype(BF16)


def expand(spec):
    per = 4
    return pl.pallas_call(
        expand_kernel,
        grid=(GROUPS // per,),
        out_shape=jax.ShapeDtypeStruct((GROUPS, 4 * CH, ROWS), BF16),
        in_specs=[pl.BlockSpec((per, ROWS, CH), lambda g: (g, 0, 0))],
        out_specs=pl.BlockSpec((per, 4 * CH, ROWS), lambda g: (g, 0, 0)),
        scratch_shapes=[pltpu.VMEM((2, 4 * CH, 128), F32)],
        compiler_params=pltpu.CompilerParams(vmem_limit_bytes=32 * 2**20),
        cost_estimate=pl.CostEstimate(flops=2**26, bytes_accessed=20 * 2**20, transcendentals=0),
        name="expand",
    )(spec)


def correlate_kernel(steps, own, partner, table, *refs):
    outs, cross = refs[:-1], refs[-1]
    step = pl.program_id(0)
    per = own.shape[0]
    sub = lax.broadcasted_iota(jnp.int32, (WIN, 8, CH), 1)

    @pl.when(step < steps)
    def _():
        for pair in range(per // 2):
            halves = []
            for half in range(2):
                part = partner[2 * pair + half]
                wide = part.astype(F32).reshape(WIN, 8, CH)
                turned = jnp.where(sub < 4, -1.0, 1.0) * pltpu.roll(wide, 4, 1)
                right = jnp.concatenate([part, turned.reshape(ROWS, CH).astype(BF16)], axis=1)
                prod = jnp.dot(own[2 * pair + half], right, preferred_element_type=F32)
                halves.append(prod.reshape(CH // 2, 8, 2 * CH))
            rows = jnp.concatenate(halves, axis=1).astype(BF16)
            first = pl.multiple_of((step * (per // 2) + pair) * 16, 16)
            cross[:, pl.ds(first, 16), :] = rows

    @pl.when(step >= steps)
    def _():
        scale = 1.0 / math.sqrt(FREQS * WIN * N_TM)
        chunk = outs[0].shape[1]
        base = (step - steps) * chunk

        def channel_pairs(idx, carry):
            first, second = cross[base + 2 * idx], cross[base + 2 * idx + 1]
            even = jnp.concatenate([first[:, :CH], second[:, :CH]], axis=1)
            odd = jnp.concatenate([first[:, CH:], second[:, CH:]], axis=1)
            even = jnp.dot(table[0], even, preferred_element_type=F32)
            odd = jnp.dot(table[1], odd, preferred_element_type=F32)
            signed = [(even + odd) * scale, (even - odd) * scale]
            for value, out in zip(signed, outs):
                value = value.astype(BF16).reshape(N_TM, 16, 2 * CH)
                out[:, 2 * idx] = value[:, :, :CH]
                out[:, 2 * idx + 1] = value[:, :, CH:]
            return carry

        lax.fori_loop(0, chunk // 2, channel_pairs, 0, unroll=2)


def correlate(own, partner, signs):
    per, chunk = 8, 16
    steps, late = GROUPS // per, CH // 2 // chunk
    return pl.pallas_call(
        functools.partial(correlate_kernel, steps),
        grid=(steps + late,),
        out_shape=[jax.ShapeDtypeStruct((N_TM, CH // 2, 16, CH), BF16)] * signs,
        in_specs=[
            pl.BlockSpec((per, 4 * CH, ROWS), lambda g: (jnp.minimum(g, steps - 1), 0, 0)),
            pl.BlockSpec((per, ROWS, CH), lambda g: (jnp.minimum(g, steps - 1), 0, 0)),
            pl.BlockSpec((2, 2 * LAGS, 2 * FREQS), lambda g: (0, 0, 0)),
        ],
        out_specs=[
            pl.BlockSpec((N_TM, chunk, 16, CH), lambda g: (0, jnp.maximum(g - steps, 0), 0, 0))
        ]
        * signs,
        scratch_shapes=[pltpu.VMEM((CH // 2, 2 * FREQS, 2 * CH), BF16)],
        compiler_params=pltpu.CompilerParams(vmem_limit_bytes=48 * 2**20),
        cost_estimate=pl.CostEstimate(flops=2**34, bytes_accessed=24 * 2**20, transcendentals=0),
        name="correlate_both" if signs == 2 else "correlate_one",
    )(own, partner, jnp.asarray(lag_rows()))


def pick_kernel(index, source, out, held, in_sems, out_sems):
    blocks = range(held.shape[0])
    into = [
        pltpu.make_async_copy(source.at[index[c]], held.at[c], in_sems.at[c]) for c in blocks
    ]
    away = [pltpu.make_async_copy(held.at[c], out.at[c], out_sems.at[c]) for c in blocks]
    for copy in into:
        copy.start()
    for arrive, leave in zip(into, away):
        arrive.wait()
        leave.start()
    for copy in away:
        copy.wait()


def pick(source, index):
    return pl.pallas_call(
        pick_kernel,
        grid_spec=pltpu.PrefetchScalarGridSpec(
            num_scalar_prefetch=1,
            grid=(1,),
            in_specs=[pl.BlockSpec(memory_space=pl.ANY)],
            out_specs=pl.BlockSpec(memory_space=pl.ANY),
            scratch_shapes=[
                pltpu.VMEM(source.shape, source.dtype),
                pltpu.SemaphoreType.DMA((source.shape[0],)),
                pltpu.SemaphoreType.DMA((source.shape[0],)),
            ],
        ),
        out_shape=jax.ShapeDtypeStruct(source.shape, source.dtype),
        compiler_params=pltpu.CompilerParams(vmem_limit_bytes=48 * 2**20),
        cost_estimate=pl.CostEstimate(
            flops=0, bytes_accessed=2 * source.size * source.dtype.itemsize, transcendentals=0
        ),
        name="pick",
    )(index, source)


def at(values, index):
    hit = index[:, None] == jnp.arange(N_CHAN, dtype=jnp.int32)[None, :]
    return jnp.sum(jnp.where(hit, values[None, :], 0), axis=1)


def orient(pairing):
    zero, one = pairing[0], pairing[1]
    hop = at(one, zero)
    least = jnp.arange(N_CHAN, dtype=jnp.int32)
    for _ in range(3):
        least = jnp.minimum(least, at(least, hop))
        hop = at(hop, hop)
    handles_zero = least < at(least, zero)
    return handles_zero, jnp.where(handles_zero, zero, one), jnp.where(handles_zero, one, zero)


def over_chan(blocks):
    return lax.all_to_all(blocks, "chan", split_axis=0, concat_axis=0, tiled=True)


def sum_over_tm(parts):
    me = lax.axis_index("tm")
    mine_x, mine_y = me // 2, me % 2
    shape = parts.shape[1:]
    parts = parts.reshape((4, 2) + shape)
    total = lax.dynamic_index_in_dim(parts, mine_x, 0, keepdims=False).astype(F32)
    got = []
    for shift in (2, 1, 3):
        block = lax.dynamic_index_in_dim(parts, (mine_x + shift) % 4, 0, keepdims=False)
        route = [(x * 2 + y, (x + shift) % 4 * 2 + y) for x in range(4) for y in range(2)]
        got.append(lax.ppermute(block, "tm", route))
    for block in got:
        total = total + block.astype(F32)
    other = lax.dynamic_index_in_dim(total, 1 - mine_y, 0, keepdims=False).astype(BF16)
    other = lax.ppermute(other, "tm", [(t, t ^ 1) for t in range(N_TM)])
    return lax.dynamic_index_in_dim(total, mine_y, 0, keepdims=False) + other.astype(F32)


def body(traces, pairing):
    spec = whiten(traces)
    spread = over_chan(spec.reshape(N_CHAN, GROUPS // N_CHAN * ROWS, CH))
    own = expand(spec)
    handles_zero, handled, other = orient(pairing)
    spread, own, handled, other = lax.optimization_barrier((spread, own, handled, other))
    first = over_chan(pick(spread, handled)).reshape(GROUPS, ROWS, CH)
    second = over_chan(pick(spread, pairing[2])).reshape(GROUPS, ROWS, CH)
    ahead, behind = correlate(own, first, 2)
    behind = sum_over_tm(behind)
    ahead = sum_over_tm(ahead)
    (last,) = correlate(own, second, 1)
    last = sum_over_tm(last)

    def lags_first(value):
        return value.reshape(CH, 8, CH).transpose(1, 0, 2)

    forward = lags_first(ahead)
    backward = behind.reshape(N_CHAN, 64, CH).astype(BF16)
    backward = over_chan(pick(over_chan(backward), other))
    backward = backward.astype(F32).reshape(CH, 8, CH).transpose(1, 2, 0)
    mine = lax.dynamic_index_in_dim(handles_zero, lax.axis_index("chan"), 0, keepdims=False)
    return jnp.stack(
        [
            jnp.where(mine, forward, backward),
            jnp.where(mine, backward, forward),
            lags_first(last),
        ]
    )


def solution(mesh):
    return jax.shard_map(
        body,
        mesh=mesh,
        in_specs=(P("chan", "tm", None), P()),
        out_specs=P(None, "tm", "chan", None),
        check_vma=False,
    )
```

```python
import functools
import math

import jax
import jax.numpy as jnp
import numpy as np
from jax import lax
from jax.experimental import pallas as pl
from jax.experimental.pallas import tpu as pltpu
from jax.sharding import PartitionSpec as P

FREQS = 256
SAMPLES = 512
LAGS = 64
CH = 128
WIN = 32
GROUPS = 64
ROWS = 256
N_CHAN = 16
N_TM = 8
WATER = 1.0
EPS = 1e-06
F32 = jnp.float32
BF16 = jnp.bfloat16


def forward_rows():
    freq = np.arange(FREQS)[:, None]
    sample = np.arange(SAMPLES)[None, :]
    phase = (freq * sample % SAMPLES) * (2.0 * math.pi / SAMPLES)
    both = np.stack([np.cos(phase), -np.sin(phase)], 0)
    both = both.reshape(2, GROUPS, 4, SAMPLES).transpose(1, 0, 2, 3)
    return both.reshape(2 * FREQS, SAMPLES).astype(np.float32).astype(BF16)


def lag_rows():
    lag = np.arange(LAGS)[:, None]
    freq = np.arange(FREQS)[None, :]
    phase = (lag * freq % SAMPLES) * (2.0 * math.pi / SAMPLES)
    both = np.stack([np.cos(phase), -np.sin(phase)], 0)
    both = both.reshape(2, N_TM, 1, 8, GROUPS, 1, 4)
    parity = np.eye(2).reshape(1, 1, 2, 1, 1, 2, 1)
    return (both * parity).reshape(2, 2 * LAGS, 2 * FREQS).astype(np.float32).astype(BF16)


def taper_row():
    pos = np.arange(SAMPLES)
    taper = 0.5 - 0.5 * np.cos((pos + 0.5) * (2.0 * math.pi / SAMPLES))
    return taper.astype(np.float32).reshape(1, SAMPLES)


def whiten_kernel(traces, taper, table, out, tapered):
    def taper_step(step, carry):
        rows = traces[pl.ds(step * 8, 8)].astype(F32)
        rows = rows - jnp.mean(rows, axis=2, keepdims=True)
        rows = (rows * taper[...].reshape(1, 1, SAMPLES)).reshape(8 * WIN, SAMPLES)
        for tile in range(4):
            tapered[tile, pl.ds(step * 8 * WIN, 8 * WIN), :] = rows[:, tile * 128 : tile * 128 + 128]
        return carry

    lax.fori_loop(0, CH // 8, taper_step, 0, unroll=2)

    def window_pair(pair, carry):
        parts = []
        for half in range(2):
            tiles = [
                tapered[tile, pl.ds(pair * 2 + half, CH, stride=WIN), :] for tile in range(4)
            ]
            parts.append(jnp.concatenate(tiles, axis=1).astype(BF16))
        columns = jnp.concatenate(parts, axis=0)
        spec = lax.dot_general(
            table[...], columns, (((1,), (1,)), ((), ())), preferred_element_type=F32
        ).reshape(GROUPS, 8, 2 * CH)
        square = spec * spec
        level = jnp.sum(jnp.sum(square, axis=0), axis=0, keepdims=True) * (1.0 / FREQS)
        power = square + pltpu.roll(square, 4, 1)
        white = spec * lax.rsqrt(power + WATER * level.reshape(1, 1, 2 * CH) + EPS)
        white = jnp.concatenate([white[:, :, :CH], white[:, :, CH:]], axis=1)
        out[:, pl.ds(pl.multiple_of(pair * 16, 16), 16), :] = white.astype(BF16)
        return carry

    lax.fori_loop(0, WIN // 2, window_pair, 0, unroll=4)


def whiten(traces):
    return pl.pallas_call(
        whiten_kernel,
        out_shape=jax.ShapeDtypeStruct((GROUPS, ROWS, CH), BF16),
        in_specs=[pl.BlockSpec(memory_space=pltpu.VMEM)] * 3,
        out_specs=pl.BlockSpec(memory_space=pltpu.VMEM),
        scratch_shapes=[pltpu.VMEM((4, CH * WIN, 128), F32)],
        compiler_params=pltpu.CompilerParams(vmem_limit_bytes=40 * 2**20),
        cost_estimate=pl.CostEstimate(flops=2 * 2**30, bytes_accessed=2**23, transcendentals=2**20),
        name="whiten",
    )(traces, jnp.asarray(taper_row()), jnp.asarray(forward_rows()))


def expand_kernel(spec, out, wide):
    lane = lax.broadcasted_iota(jnp.int32, (CH, ROWS), 1)
    for part in range(spec.shape[0]):
        turned = spec[part].astype(F32).T
        for f in range(4):
            kept = jnp.where(lane % 4 == f, turned, 0.0)
            for tile in range(2):
                wide[tile, pl.ds(f, CH, stride=4), :] = kept[:, tile * 128 : tile * 128 + 128]
        for tile in range(2):
            out[part, :, tile * 128 : tile * 128 + 128] = wide[tile].astype(BF16)


def expand(spec):
    per = 4
    return pl.pallas_call(
        expand_kernel,
        grid=(GROUPS // per,),
        out_shape=jax.ShapeDtypeStruct((GROUPS, 4 * CH, ROWS), BF16),
        in_specs=[pl.BlockSpec((per, ROWS, CH), lambda g: (g, 0, 0))],
        out_specs=pl.BlockSpec((per, 4 * CH, ROWS), lambda g: (g, 0, 0)),
        scratch_shapes=[pltpu.VMEM((2, 4 * CH, 128), F32)],
        compiler_params=pltpu.CompilerParams(vmem_limit_bytes=32 * 2**20),
        cost_estimate=pl.CostEstimate(flops=2**26, bytes_accessed=20 * 2**20, transcendentals=0),
        name="expand",
    )(spec)


def correlate_kernel(steps, own_hbm, partner_hbm, table, *refs):
    outs = refs[:4]
    own, partner, cross, own_sems, partner_sems = refs[4:]
    step = pl.program_id(0)
    per = GROUPS // steps
    sub = lax.broadcasted_iota(jnp.int32, (WIN, 8, CH), 1)

    def arrivals(chunk):
        groups = pl.ds(chunk * per, per)
        return (
            pltpu.make_async_copy(own_hbm.at[groups], own.at[groups], own_sems.at[chunk]),
            pltpu.make_async_copy(
                partner_hbm.at[groups], partner.at[groups], partner_sems.at[chunk]
            ),
        )

    @pl.when(step == 0)
    def _():
        for chunk in range(steps):
            for copy in arrivals(chunk):
                copy.start()

    @pl.when(step < steps)
    def _():
        for copy in arrivals(step):
            copy.wait()
        for pair in range(per // 2):
            halves = []
            for half in range(2):
                group = step * per + 2 * pair + half
                part = partner[group]
                wide = part.astype(F32).reshape(WIN, 8, CH)
                turned = jnp.where(sub < 4, -1.0, 1.0) * pltpu.roll(wide, 4, 1)
                right = jnp.concatenate([part, turned.reshape(ROWS, CH).astype(BF16)], axis=1)
                prod = jnp.dot(own[group], right, preferred_element_type=F32)
                halves.append(prod.reshape(CH // 2, 8, 2 * CH))
            rows = jnp.concatenate(halves, axis=1).astype(BF16)
            first = pl.multiple_of((step * (per // 2) + pair) * 16, 16)
            cross[:, pl.ds(first, 16), :] = rows

    @pl.when(step >= steps)
    def _():
        scale = 1.0 / math.sqrt(FREQS * WIN * N_TM)
        signs, chunk = outs[0].shape[1:3]
        base = (step - steps) * chunk

        def channel_pairs(idx, carry):
            first, second = cross[base + 2 * idx], cross[base + 2 * idx + 1]
            even = jnp.concatenate([first[:, :CH], second[:, :CH]], axis=1)
            odd = jnp.concatenate([first[:, CH:], second[:, CH:]], axis=1)
            even = jnp.dot(table[0], even, preferred_element_type=F32)
            odd = jnp.dot(table[1], odd, preferred_element_type=F32)
            for sign in range(signs):
                value = (even - odd if sign else even + odd) * scale
                value = value.astype(BF16).reshape(4, 2, 16, 2 * CH)
                for shift in range(4):
                    outs[shift][:, sign, 2 * idx] = value[shift, :, :, :CH]
                    outs[shift][:, sign, 2 * idx + 1] = value[shift, :, :, CH:]
            return carry

        lax.fori_loop(0, chunk // 2, channel_pairs, 0, unroll=2)


def correlate(own, partner, table, signs):
    per, chunk = 8, 16
    steps, late = GROUPS // per, CH // 2 // chunk
    block = pl.BlockSpec(
        (2, signs, chunk, 16, CH), lambda g: (0, 0, jnp.maximum(g - steps, 0), 0, 0)
    )
    return pl.pallas_call(
        functools.partial(correlate_kernel, steps),
        grid=(steps + late,),
        out_shape=[jax.ShapeDtypeStruct((2, signs, CH // 2, 16, CH), BF16)] * 4,
        in_specs=[
            pl.BlockSpec(memory_space=pl.ANY),
            pl.BlockSpec(memory_space=pl.ANY),
            pl.BlockSpec((2, 2 * LAGS, 2 * FREQS), lambda g: (0, 0, 0)),
        ],
        out_specs=[block] * 4,
        scratch_shapes=[
            pltpu.VMEM((GROUPS, 4 * CH, ROWS), BF16),
            pltpu.VMEM((GROUPS, ROWS, CH), BF16),
            pltpu.VMEM((CH // 2, 2 * FREQS, 2 * CH), BF16),
            pltpu.SemaphoreType.DMA((steps,)),
            pltpu.SemaphoreType.DMA((steps,)),
        ],
        compiler_params=pltpu.CompilerParams(vmem_limit_bytes=56 * 2**20),
        cost_estimate=pl.CostEstimate(flops=2**34, bytes_accessed=24 * 2**20, transcendentals=0),
        name="correlate_both" if signs == 2 else "correlate_one",
    )(own, partner, table)


def pick_kernel(index, source, out, held, in_sems, out_sems):
    blocks = range(held.shape[0])
    into = [
        pltpu.make_async_copy(source.at[index[c]], held.at[c], in_sems.at[c]) for c in blocks
    ]
    away = [pltpu.make_async_copy(held.at[c], out.at[c], out_sems.at[c]) for c in blocks]
    for copy in into:
        copy.start()
    for arrive, leave in zip(into, away):
        arrive.wait()
        leave.start()
    for copy in away:
        copy.wait()


def pick(source, index):
    return pl.pallas_call(
        pick_kernel,
        grid_spec=pltpu.PrefetchScalarGridSpec(
            num_scalar_prefetch=1,
            grid=(1,),
            in_specs=[pl.BlockSpec(memory_space=pltpu.HBM)],
            out_specs=pl.BlockSpec(memory_space=pltpu.HBM),
            scratch_shapes=[
                pltpu.VMEM(source.shape, source.dtype),
                pltpu.SemaphoreType.DMA((source.shape[0],)),
                pltpu.SemaphoreType.DMA((source.shape[0],)),
            ],
        ),
        out_shape=jax.ShapeDtypeStruct(source.shape, source.dtype),
        compiler_params=pltpu.CompilerParams(vmem_limit_bytes=58 * 2**20),
        cost_estimate=pl.CostEstimate(
            flops=0, bytes_accessed=2 * source.size * source.dtype.itemsize, transcendentals=0
        ),
        name="pick",
    )(index, source)


def at(values, index):
    hit = index[:, None] == jnp.arange(N_CHAN, dtype=jnp.int32)[None, :]
    return jnp.sum(jnp.where(hit, values[None, :], 0), axis=1)


def orient(pairing):
    zero, one = pairing[0], pairing[1]
    hop = at(one, zero)
    least = jnp.arange(N_CHAN, dtype=jnp.int32)
    for _ in range(3):
        least = jnp.minimum(least, at(least, hop))
        hop = at(hop, hop)
    handles_zero = least < at(least, zero)
    return handles_zero, jnp.where(handles_zero, zero, one), jnp.where(handles_zero, one, zero)


def over_chan(blocks):
    return lax.all_to_all(blocks, "chan", split_axis=0, concat_axis=0, tiled=True)


def sent_over_x(parts):
    got = [parts[0]]
    for shift in (2, 1, 3):
        route = [(x * 2 + y, (x + shift) % 4 * 2 + y) for x in range(4) for y in range(2)]
        got.append(lax.ppermute(parts[shift], "tm", route))
    return got


def sum_of(blocks):
    total = blocks[0].astype(F32)
    for block in blocks[1:]:
        total = total + block.astype(F32)
    return total


def sum_over_y(halves):
    mine = lax.axis_index("tm") % 2
    other = lax.dynamic_index_in_dim(halves, 1 - mine, 0, keepdims=False).astype(BF16)
    other = lax.ppermute(other, "tm", [(t, t ^ 1) for t in range(N_TM)])
    return lax.dynamic_index_in_dim(halves, mine, 0, keepdims=False) + other.astype(F32)


def body(traces, pairing):
    spec = whiten(traces)
    spread = over_chan(spec.reshape(N_CHAN, GROUPS // N_CHAN * ROWS, CH))
    own = expand(spec)
    handles_zero, handled, other = orient(pairing)
    table = jnp.asarray(np.concatenate([lag_rows()] * 2, axis=1))
    table = lax.dynamic_slice_in_dim(table, lax.axis_index("tm") // 2 * 32, 2 * LAGS, 1)
    spread, own, handled, other, table = lax.optimization_barrier(
        (spread, own, handled, other, table)
    )
    first = over_chan(pick(spread, handled)).reshape(GROUPS, ROWS, CH)
    second = over_chan(pick(spread, pairing[2])).reshape(GROUPS, ROWS, CH)
    pair_halves = sum_of(sent_over_x(correlate(own, first, table, 2)))
    last_blocks = sent_over_x(correlate(own, second, table, 1))
    behind = sum_over_y(pair_halves[:, 1])
    behind = over_chan(behind.reshape(N_CHAN, 64, CH).astype(BF16))
    behind, last_blocks = lax.optimization_barrier((behind, last_blocks))
    behind = over_chan(pick(behind, other))
    ahead = sum_over_y(pair_halves[:, 0])
    last = sum_over_y(sum_of(last_blocks)[:, 0])

    def lags_first(value):
        return value.reshape(CH, 8, CH).transpose(1, 0, 2)

    forward = lags_first(ahead)
    backward = behind.astype(F32).reshape(CH, 8, CH).transpose(1, 2, 0)
    mine = lax.dynamic_index_in_dim(handles_zero, lax.axis_index("chan"), 0, keepdims=False)
    return jnp.stack(
        [
            jnp.where(mine, forward, backward),
            jnp.where(mine, backward, forward),
            lags_first(last),
        ]
    )


def solution(mesh):
    return jax.shard_map(
        body,
        mesh=mesh,
        in_specs=(P("chan", "tm", None), P()),
        out_specs=P(None, "tm", "chan", None),
        check_vma=False,
    )
```

```python
import functools
import math

import jax
import jax.numpy as jnp
import numpy as np
from jax import lax
from jax.experimental import pallas as pl
from jax.experimental.pallas import tpu as pltpu
from jax.sharding import PartitionSpec as P

FREQS = 256
SAMPLES = 512
LAGS = 64
CH = 128
WIN = 32
GROUPS = 64
ROWS = 256
N_CHAN = 16
N_TM = 8
WATER = 1.0
EPS = 1e-06
F32 = jnp.float32
BF16 = jnp.bfloat16


def forward_rows():
    freq = np.arange(FREQS)[:, None]
    sample = np.arange(SAMPLES)[None, :]
    phase = (freq * sample % SAMPLES) * (2.0 * math.pi / SAMPLES)
    both = np.stack([np.cos(phase), -np.sin(phase)], 0)
    both = both.reshape(2, GROUPS, 4, SAMPLES).transpose(1, 0, 2, 3)
    return both.reshape(2 * FREQS, SAMPLES).astype(np.float32).astype(BF16)


def lag_rows():
    lag = np.arange(LAGS)[:, None]
    freq = np.arange(FREQS)[None, :]
    phase = (lag * freq % SAMPLES) * (2.0 * math.pi / SAMPLES)
    both = np.stack([np.cos(phase), -np.sin(phase)], 0)
    both = both.reshape(2, N_TM, 1, 8, GROUPS, 1, 4)
    parity = np.eye(2).reshape(1, 1, 2, 1, 1, 2, 1)
    return (both * parity).reshape(2, 2 * LAGS, 2 * FREQS).astype(np.float32).astype(BF16)


def taper_row():
    pos = np.arange(SAMPLES)
    taper = 0.5 - 0.5 * np.cos((pos + 0.5) * (2.0 * math.pi / SAMPLES))
    return taper.astype(np.float32).reshape(1, SAMPLES)


CHUNK = 16
PART = 4


def whiten_kernel(
    traces, taper_hbm, table_hbm, out, raw, taper, table, tapered, white_rows, small_sems, in_sems, out_sems
):
    taper_copy = pltpu.make_async_copy(taper_hbm, taper, small_sems.at[0])
    table_copy = pltpu.make_async_copy(table_hbm, table, small_sems.at[1])

    def arrival(chunk):
        rows = pl.ds(chunk * CHUNK, CHUNK)
        return pltpu.make_async_copy(traces.at[rows], raw.at[rows], in_sems.at[chunk])

    def departure(part):
        rows = pl.ds(pl.multiple_of(part * PART * 16, PART * 16), PART * 16)
        return pltpu.make_async_copy(
            white_rows.at[:, rows, :], out.at[:, rows, :], out_sems.at[part]
        )

    taper_copy.start()
    for chunk in range(CH // CHUNK):
        arrival(chunk).start()
    table_copy.start()
    taper_copy.wait()

    def taper_step(chunk, carry):
        arrival(chunk).wait()
        for half in range(CHUNK // 8):
            first = chunk * CHUNK + half * 8
            rows = raw[pl.ds(first, 8)].astype(F32)
            rows = rows - jnp.mean(rows, axis=2, keepdims=True)
            rows = (rows * taper[...].reshape(1, 1, SAMPLES)).reshape(8 * WIN, SAMPLES)
            for tile in range(4):
                tapered[tile, pl.ds(first * WIN, 8 * WIN), :] = rows[:, tile * 128 : tile * 128 + 128]
        return carry

    lax.fori_loop(0, CH // CHUNK, taper_step, 0)
    table_copy.wait()

    def window_pairs(part, carry):
        for pair in [part * PART + inner for inner in range(PART)]:
            columns = []
            for half in range(2):
                tiles = [
                    tapered[tile, pl.ds(pair * 2 + half, CH, stride=WIN), :] for tile in range(4)
                ]
                columns.append(jnp.concatenate(tiles, axis=1).astype(BF16))
            columns = jnp.concatenate(columns, axis=0)
            spec = lax.dot_general(
                table[...], columns, (((1,), (1,)), ((), ())), preferred_element_type=F32
            ).reshape(GROUPS, 8, 2 * CH)
            square = spec * spec
            level = jnp.sum(jnp.sum(square, axis=0), axis=0, keepdims=True) * (1.0 / FREQS)
            power = square + pltpu.roll(square, 4, 1)
            white = spec * lax.rsqrt(power + WATER * level.reshape(1, 1, 2 * CH) + EPS)
            white = jnp.concatenate([white[:, :, :CH], white[:, :, CH:]], axis=1)
            white_rows[:, pl.ds(pl.multiple_of(pair * 16, 16), 16), :] = white.astype(BF16)
        departure(part).start()
        return carry

    lax.fori_loop(0, WIN // 2 // PART, window_pairs, 0)
    for part in range(WIN // 2 // PART):
        departure(part).wait()


def whiten(traces):
    return pl.pallas_call(
        whiten_kernel,
        out_shape=jax.ShapeDtypeStruct((GROUPS, ROWS, CH), BF16),
        in_specs=[pl.BlockSpec(memory_space=pl.ANY)] * 3,
        out_specs=pl.BlockSpec(memory_space=pl.ANY),
        scratch_shapes=[
            pltpu.VMEM((CH, WIN, SAMPLES), BF16),
            pltpu.VMEM((1, SAMPLES), F32),
            pltpu.VMEM((2 * FREQS, SAMPLES), BF16),
            pltpu.VMEM((4, CH * WIN, 128), F32),
            pltpu.VMEM((GROUPS, ROWS, CH), BF16),
            pltpu.SemaphoreType.DMA((2,)),
            pltpu.SemaphoreType.DMA((CH // CHUNK,)),
            pltpu.SemaphoreType.DMA((WIN // 2 // PART,)),
        ],
        compiler_params=pltpu.CompilerParams(vmem_limit_bytes=60 * 2**20),
        cost_estimate=pl.CostEstimate(flops=2 * 2**30, bytes_accessed=2**23, transcendentals=2**20),
        name="whiten",
    )(traces, jnp.asarray(taper_row()), jnp.asarray(forward_rows()))


def expand_kernel(spec, out, wide):
    lane = lax.broadcasted_iota(jnp.int32, (CH, ROWS), 1)
    for part in range(spec.shape[0]):
        turned = spec[part].astype(F32).T
        for f in range(4):
            kept = jnp.where(lane % 4 == f, turned, 0.0)
            for tile in range(2):
                wide[tile, pl.ds(f, CH, stride=4), :] = kept[:, tile * 128 : tile * 128 + 128]
        for tile in range(2):
            out[part, :, tile * 128 : tile * 128 + 128] = wide[tile].astype(BF16)


def expand(spec):
    per = 4
    return pl.pallas_call(
        expand_kernel,
        grid=(GROUPS // per,),
        out_shape=jax.ShapeDtypeStruct((GROUPS, 4 * CH, ROWS), BF16),
        in_specs=[pl.BlockSpec((per, ROWS, CH), lambda g: (g, 0, 0))],
        out_specs=pl.BlockSpec((per, 4 * CH, ROWS), lambda g: (g, 0, 0)),
        scratch_shapes=[pltpu.VMEM((2, 4 * CH, 128), F32)],
        compiler_params=pltpu.CompilerParams(vmem_limit_bytes=32 * 2**20),
        cost_estimate=pl.CostEstimate(flops=2**26, bytes_accessed=20 * 2**20, transcendentals=0),
        name="expand",
    )(spec)


def correlate_kernel(steps, own_hbm, partner_hbm, table, *refs):
    outs = refs[:4]
    own, partner, cross, own_sems, partner_sems = refs[4:]
    step = pl.program_id(0)
    per = GROUPS // steps
    sub = lax.broadcasted_iota(jnp.int32, (WIN, 8, CH), 1)

    def arrivals(chunk):
        groups = pl.ds(chunk * per, per)
        return (
            pltpu.make_async_copy(own_hbm.at[groups], own.at[groups], own_sems.at[chunk]),
            pltpu.make_async_copy(
                partner_hbm.at[groups], partner.at[groups], partner_sems.at[chunk]
            ),
        )

    @pl.when(step == 0)
    def _():
        for chunk in range(steps):
            for copy in arrivals(chunk):
                copy.start()

    @pl.when(step < steps)
    def _():
        for copy in arrivals(step):
            copy.wait()
        for pair in range(per // 2):
            halves = []
            for half in range(2):
                group = step * per + 2 * pair + half
                part = partner[group]
                wide = part.astype(F32).reshape(WIN, 8, CH)
                turned = jnp.where(sub < 4, -1.0, 1.0) * pltpu.roll(wide, 4, 1)
                right = jnp.concatenate([part, turned.reshape(ROWS, CH).astype(BF16)], axis=1)
                prod = jnp.dot(own[group], right, preferred_element_type=F32)
                halves.append(prod.reshape(CH // 2, 8, 2 * CH))
            rows = jnp.concatenate(halves, axis=1).astype(BF16)
            first = pl.multiple_of((step * (per // 2) + pair) * 16, 16)
            cross[:, pl.ds(first, 16), :] = rows

    @pl.when(step >= steps)
    def _():
        scale = 1.0 / math.sqrt(FREQS * WIN * N_TM)
        signs, chunk = outs[0].shape[1:3]
        base = (step - steps) * chunk

        def channel_pairs(idx, carry):
            first, second = cross[base + 2 * idx], cross[base + 2 * idx + 1]
            even = jnp.concatenate([first[:, :CH], second[:, :CH]], axis=1)
            odd = jnp.concatenate([first[:, CH:], second[:, CH:]], axis=1)
            even = jnp.dot(table[0], even, preferred_element_type=F32)
            odd = jnp.dot(table[1], odd, preferred_element_type=F32)
            for sign in range(signs):
                value = (even - odd if sign else even + odd) * scale
                value = value.astype(BF16).reshape(4, 2, 16, 2 * CH)
                for shift in range(4):
                    outs[shift][:, sign, 2 * idx] = value[shift, :, :, :CH]
                    outs[shift][:, sign, 2 * idx + 1] = value[shift, :, :, CH:]
            return carry

        lax.fori_loop(0, chunk // 2, channel_pairs, 0, unroll=2)


def correlate(own, partner, table, signs):
    per, chunk = 8, 16
    steps, late = GROUPS // per, CH // 2 // chunk
    block = pl.BlockSpec(
        (2, signs, chunk, 16, CH), lambda g: (0, 0, jnp.maximum(g - steps, 0), 0, 0)
    )
    return pl.pallas_call(
        functools.partial(correlate_kernel, steps),
        grid=(steps + late,),
        out_shape=[jax.ShapeDtypeStruct((2, signs, CH // 2, 16, CH), BF16)] * 4,
        in_specs=[
            pl.BlockSpec(memory_space=pl.ANY),
            pl.BlockSpec(memory_space=pl.ANY),
            pl.BlockSpec((2, 2 * LAGS, 2 * FREQS), lambda g: (0, 0, 0)),
        ],
        out_specs=[block] * 4,
        scratch_shapes=[
            pltpu.VMEM((GROUPS, 4 * CH, ROWS), BF16),
            pltpu.VMEM((GROUPS, ROWS, CH), BF16),
            pltpu.VMEM((CH // 2, 2 * FREQS, 2 * CH), BF16),
            pltpu.SemaphoreType.DMA((steps,)),
            pltpu.SemaphoreType.DMA((steps,)),
        ],
        compiler_params=pltpu.CompilerParams(vmem_limit_bytes=56 * 2**20),
        cost_estimate=pl.CostEstimate(flops=2**34, bytes_accessed=24 * 2**20, transcendentals=0),
        name="correlate_both" if signs == 2 else "correlate_one",
    )(own, partner, table)


def pick_kernel(index, source, out, held, in_sems, out_sems):
    blocks = range(held.shape[0])
    into = [
        pltpu.make_async_copy(source.at[index[c]], held.at[c], in_sems.at[c]) for c in blocks
    ]
    away = [pltpu.make_async_copy(held.at[c], out.at[c], out_sems.at[c]) for c in blocks]
    for copy in into:
        copy.start()
    for arrive, leave in zip(into, away):
        arrive.wait()
        leave.start()
    for copy in away:
        copy.wait()


def pick(source, index):
    return pl.pallas_call(
        pick_kernel,
        grid_spec=pltpu.PrefetchScalarGridSpec(
            num_scalar_prefetch=1,
            grid=(1,),
            in_specs=[pl.BlockSpec(memory_space=pltpu.HBM)],
            out_specs=pl.BlockSpec(memory_space=pltpu.HBM),
            scratch_shapes=[
                pltpu.VMEM(source.shape, source.dtype),
                pltpu.SemaphoreType.DMA((source.shape[0],)),
                pltpu.SemaphoreType.DMA((source.shape[0],)),
            ],
        ),
        out_shape=jax.ShapeDtypeStruct(source.shape, source.dtype),
        compiler_params=pltpu.CompilerParams(vmem_limit_bytes=58 * 2**20),
        cost_estimate=pl.CostEstimate(
            flops=0, bytes_accessed=2 * source.size * source.dtype.itemsize, transcendentals=0
        ),
        name="pick",
    )(index, source)


def at(values, index):
    hit = index[:, None] == jnp.arange(N_CHAN, dtype=jnp.int32)[None, :]
    return jnp.sum(jnp.where(hit, values[None, :], 0), axis=1)


def orient(pairing):
    zero, one = pairing[0], pairing[1]
    hop = at(one, zero)
    least = jnp.arange(N_CHAN, dtype=jnp.int32)
    for _ in range(3):
        least = jnp.minimum(least, at(least, hop))
        hop = at(hop, hop)
    handles_zero = least < at(least, zero)
    return handles_zero, jnp.where(handles_zero, zero, one), jnp.where(handles_zero, one, zero)


def over_chan(blocks):
    return lax.all_to_all(blocks, "chan", split_axis=0, concat_axis=0, tiled=True)


def sent_over_x(parts):
    got = [parts[0]]
    for shift in (2, 1, 3):
        route = [(x * 2 + y, (x + shift) % 4 * 2 + y) for x in range(4) for y in range(2)]
        got.append(lax.ppermute(parts[shift], "tm", route))
    return got


def sum_of(blocks):
    total = blocks[0].astype(F32)
    for block in blocks[1:]:
        total = total + block.astype(F32)
    return total


def sum_over_y(halves):
    mine = lax.axis_index("tm") % 2
    other = lax.dynamic_index_in_dim(halves, 1 - mine, 0, keepdims=False).astype(BF16)
    other = lax.ppermute(other, "tm", [(t, t ^ 1) for t in range(N_TM)])
    return lax.dynamic_index_in_dim(halves, mine, 0, keepdims=False) + other.astype(F32)


def body(traces, pairing):
    spec = whiten(traces)
    spread = over_chan(spec.reshape(N_CHAN, GROUPS // N_CHAN * ROWS, CH))
    own = expand(spec)
    handles_zero, handled, other = orient(pairing)
    table = jnp.asarray(np.concatenate([lag_rows()] * 2, axis=1))
    table = lax.dynamic_slice_in_dim(table, lax.axis_index("tm") // 2 * 32, 2 * LAGS, 1)
    spread, own, handled, other, table = lax.optimization_barrier(
        (spread, own, handled, other, table)
    )
    first = over_chan(pick(spread, handled)).reshape(GROUPS, ROWS, CH)
    second = over_chan(pick(spread, pairing[2])).reshape(GROUPS, ROWS, CH)
    pair_blocks = sent_over_x(correlate(own, first, table, 2))
    last_parts = correlate(own, second, table, 1)
    pair_blocks, last_parts = lax.optimization_barrier((pair_blocks, last_parts))
    pair_halves = sum_of(pair_blocks)
    last_blocks = sent_over_x(last_parts)
    behind = sum_over_y(pair_halves[:, 1])
    behind = over_chan(behind.reshape(N_CHAN, 64, CH).astype(BF16))
    behind, last_blocks = lax.optimization_barrier((behind, last_blocks))
    behind = over_chan(pick(behind, other))
    ahead = sum_over_y(pair_halves[:, 0])
    last = sum_over_y(sum_of(last_blocks)[:, 0])

    def lags_first(value):
        return value.reshape(CH, 8, CH).transpose(1, 0, 2)

    forward = lags_first(ahead)
    backward = behind.astype(F32).reshape(CH, 8, CH).transpose(1, 2, 0)
    mine = lax.dynamic_index_in_dim(handles_zero, lax.axis_index("chan"), 0, keepdims=False)
    return jnp.stack(
        [
            jnp.where(mine, forward, backward),
            jnp.where(mine, backward, forward),
            lags_first(last),
        ]
    )


def solution(mesh):
    return jax.shard_map(
        body,
        mesh=mesh,
        in_specs=(P("chan", "tm", None), P()),
        out_specs=P(None, "tm", "chan", None),
        check_vma=False,
    )
```

```python
import functools
import math

import jax
import jax.numpy as jnp
import numpy as np
from jax import lax
from jax.experimental import pallas as pl
from jax.experimental.pallas import tpu as pltpu
from jax.sharding import PartitionSpec as P

FREQS = 256
SAMPLES = 512
LAGS = 64
CH = 128
WIN = 32
GROUPS = 64
ROWS = 256
N_CHAN = 16
N_TM = 8
WATER = 1.0
EPS = 1e-06
F32 = jnp.float32
BF16 = jnp.bfloat16


def forward_rows():
    freq = np.arange(FREQS)[:, None]
    sample = np.arange(SAMPLES)[None, :]
    phase = (freq * sample % SAMPLES) * (2.0 * math.pi / SAMPLES)
    both = np.stack([np.cos(phase), -np.sin(phase)], 0)
    both = both.reshape(2, GROUPS, 4, SAMPLES).transpose(1, 0, 2, 3)
    return both.reshape(2 * FREQS, SAMPLES).astype(np.float32).astype(BF16)


def lag_rows():
    lag = np.arange(LAGS)[:, None]
    freq = np.arange(FREQS)[None, :]
    phase = (lag * freq % SAMPLES) * (2.0 * math.pi / SAMPLES)
    both = np.stack([np.cos(phase), -np.sin(phase)], 0)
    both = both.reshape(2, N_TM, 1, 8, GROUPS, 1, 4)
    parity = np.eye(2).reshape(1, 1, 2, 1, 1, 2, 1)
    return (both * parity).reshape(2, 2 * LAGS, 2 * FREQS).astype(np.float32).astype(BF16)


def taper_row():
    pos = np.arange(SAMPLES)
    taper = 0.5 - 0.5 * np.cos((pos + 0.5) * (2.0 * math.pi / SAMPLES))
    return taper.astype(np.float32).reshape(1, SAMPLES)


CHUNK = 16
PART = 4


def whiten_kernel(
    traces, taper_hbm, table_hbm, out, raw, taper, table, tapered, white_rows, small_sems, in_sems, out_sems
):
    taper_copy = pltpu.make_async_copy(taper_hbm, taper, small_sems.at[0])
    table_copy = pltpu.make_async_copy(table_hbm, table, small_sems.at[1])

    def arrival(chunk):
        rows = pl.ds(chunk * CHUNK, CHUNK)
        return pltpu.make_async_copy(traces.at[rows], raw.at[rows], in_sems.at[chunk])

    def departure(part):
        rows = pl.ds(pl.multiple_of(part * PART * 16, PART * 16), PART * 16)
        return pltpu.make_async_copy(
            white_rows.at[:, rows, :], out.at[:, rows, :], out_sems.at[part]
        )

    taper_copy.start()
    for chunk in range(CH // CHUNK):
        arrival(chunk).start()
    table_copy.start()
    taper_copy.wait()

    def taper_step(chunk, carry):
        arrival(chunk).wait()
        for half in range(CHUNK // 8):
            first = chunk * CHUNK + half * 8
            rows = raw[pl.ds(first, 8)].astype(F32)
            rows = rows - jnp.mean(rows, axis=2, keepdims=True)
            rows = (rows * taper[...].reshape(1, 1, SAMPLES)).reshape(8 * WIN, SAMPLES)
            for tile in range(4):
                tapered[tile, pl.ds(first * WIN, 8 * WIN), :] = rows[:, tile * 128 : tile * 128 + 128]
        return carry

    lax.fori_loop(0, CH // CHUNK, taper_step, 0)
    table_copy.wait()

    def window_pairs(part, carry):
        for pair in [part * PART + inner for inner in range(PART)]:
            columns = []
            for half in range(2):
                tiles = [
                    tapered[tile, pl.ds(pair * 2 + half, CH, stride=WIN), :] for tile in range(4)
                ]
                columns.append(jnp.concatenate(tiles, axis=1).astype(BF16))
            columns = jnp.concatenate(columns, axis=0)
            spec = lax.dot_general(
                table[...], columns, (((1,), (1,)), ((), ())), preferred_element_type=F32
            ).reshape(GROUPS, 8, 2 * CH)
            square = spec * spec
            level = jnp.sum(jnp.sum(square, axis=0), axis=0, keepdims=True) * (1.0 / FREQS)
            power = square + pltpu.roll(square, 4, 1)
            white = spec * lax.rsqrt(power + (WATER * level + EPS).reshape(1, 1, 2 * CH))
            white = jnp.concatenate([white[:, :, :CH], white[:, :, CH:]], axis=1)
            white_rows[:, pl.ds(pl.multiple_of(pair * 16, 16), 16), :] = white.astype(BF16)
        departure(part).start()
        return carry

    lax.fori_loop(0, WIN // 2 // PART, window_pairs, 0)
    for part in range(WIN // 2 // PART):
        departure(part).wait()


def whiten(traces):
    return pl.pallas_call(
        whiten_kernel,
        out_shape=jax.ShapeDtypeStruct((GROUPS, ROWS, CH), BF16),
        in_specs=[pl.BlockSpec(memory_space=pl.ANY)] * 3,
        out_specs=pl.BlockSpec(memory_space=pl.ANY),
        scratch_shapes=[
            pltpu.VMEM((CH, WIN, SAMPLES), BF16),
            pltpu.VMEM((1, SAMPLES), F32),
            pltpu.VMEM((2 * FREQS, SAMPLES), BF16),
            pltpu.VMEM((4, CH * WIN, 128), F32),
            pltpu.VMEM((GROUPS, ROWS, CH), BF16),
            pltpu.SemaphoreType.DMA((2,)),
            pltpu.SemaphoreType.DMA((CH // CHUNK,)),
            pltpu.SemaphoreType.DMA((WIN // 2 // PART,)),
        ],
        compiler_params=pltpu.CompilerParams(vmem_limit_bytes=60 * 2**20),
        cost_estimate=pl.CostEstimate(flops=2 * 2**30, bytes_accessed=2**23, transcendentals=2**20),
        name="whiten",
    )(traces, jnp.asarray(taper_row()), jnp.asarray(forward_rows()))


def expand_kernel(spec, out, wide):
    lane = lax.broadcasted_iota(jnp.int32, (CH, ROWS), 1)
    for part in range(spec.shape[0]):
        turned = spec[part].astype(F32).T
        for f in range(4):
            kept = jnp.where(lane % 4 == f, turned, 0.0)
            for tile in range(2):
                wide[tile, pl.ds(f, CH, stride=4), :] = kept[:, tile * 128 : tile * 128 + 128]
        for tile in range(2):
            out[part, :, tile * 128 : tile * 128 + 128] = wide[tile].astype(BF16)


def expand(spec):
    per = 4
    return pl.pallas_call(
        expand_kernel,
        grid=(GROUPS // per,),
        out_shape=jax.ShapeDtypeStruct((GROUPS, 4 * CH, ROWS), BF16),
        in_specs=[pl.BlockSpec((per, ROWS, CH), lambda g: (g, 0, 0))],
        out_specs=pl.BlockSpec((per, 4 * CH, ROWS), lambda g: (g, 0, 0)),
        scratch_shapes=[pltpu.VMEM((2, 4 * CH, 128), F32)],
        compiler_params=pltpu.CompilerParams(vmem_limit_bytes=32 * 2**20),
        cost_estimate=pl.CostEstimate(flops=2**26, bytes_accessed=20 * 2**20, transcendentals=0),
        name="expand",
    )(spec)


def correlate_kernel(steps, own_hbm, partner_hbm, table, *refs):
    outs = refs[:4]
    own, partner, cross, own_sems, partner_sems = refs[4:]
    step = pl.program_id(0)
    per = GROUPS // steps
    sub = lax.broadcasted_iota(jnp.int32, (WIN, 8, CH), 1)

    def arrivals(chunk):
        groups = pl.ds(chunk * per, per)
        return (
            pltpu.make_async_copy(own_hbm.at[groups], own.at[groups], own_sems.at[chunk]),
            pltpu.make_async_copy(
                partner_hbm.at[groups], partner.at[groups], partner_sems.at[chunk]
            ),
        )

    @pl.when(step == 0)
    def _():
        for chunk in range(steps):
            for copy in arrivals(chunk):
                copy.start()

    @pl.when(step < steps)
    def _():
        for copy in arrivals(step):
            copy.wait()
        for pair in range(per // 2):
            halves = []
            for half in range(2):
                group = step * per + 2 * pair + half
                part = partner[group]
                wide = part.astype(F32).reshape(WIN, 8, CH)
                turned = jnp.where(sub < 4, -1.0, 1.0) * pltpu.roll(wide, 4, 1)
                right = jnp.concatenate([part, turned.reshape(ROWS, CH).astype(BF16)], axis=1)
                prod = jnp.dot(own[group], right, preferred_element_type=F32)
                halves.append(prod.reshape(CH // 2, 8, 2 * CH))
            rows = jnp.concatenate(halves, axis=1).astype(BF16)
            first = pl.multiple_of((step * (per // 2) + pair) * 16, 16)
            cross[:, pl.ds(first, 16), :] = rows

    @pl.when(step >= steps)
    def _():
        scale = 1.0 / math.sqrt(FREQS * WIN * N_TM)
        signs, chunk = outs[0].shape[1:3]
        base = (step - steps) * chunk

        def channel_pairs(idx, carry):
            first, second = cross[base + 2 * idx], cross[base + 2 * idx + 1]
            even = jnp.concatenate([first[:, :CH], second[:, :CH]], axis=1)
            odd = jnp.concatenate([first[:, CH:], second[:, CH:]], axis=1)
            even = jnp.dot(table[0], even, preferred_element_type=F32)
            odd = jnp.dot(table[1], odd, preferred_element_type=F32)
            for sign in range(signs):
                value = (even - odd if sign else even + odd) * scale
                value = value.astype(BF16).reshape(4, 2, 16, 2 * CH)
                for shift in range(4):
                    outs[shift][:, sign, 2 * idx] = value[shift, :, :, :CH]
                    outs[shift][:, sign, 2 * idx + 1] = value[shift, :, :, CH:]
            return carry

        lax.fori_loop(0, chunk // 2, channel_pairs, 0, unroll=8)


def correlate(own, partner, table, signs):
    per, chunk = 8, 16
    steps, late = GROUPS // per, CH // 2 // chunk
    block = pl.BlockSpec(
        (2, signs, chunk, 16, CH), lambda g: (0, 0, jnp.maximum(g - steps, 0), 0, 0)
    )
    return pl.pallas_call(
        functools.partial(correlate_kernel, steps),
        grid=(steps + late,),
        out_shape=[jax.ShapeDtypeStruct((2, signs, CH // 2, 16, CH), BF16)] * 4,
        in_specs=[
            pl.BlockSpec(memory_space=pl.ANY),
            pl.BlockSpec(memory_space=pl.ANY),
            pl.BlockSpec((2, 2 * LAGS, 2 * FREQS), lambda g: (0, 0, 0)),
        ],
        out_specs=[block] * 4,
        scratch_shapes=[
            pltpu.VMEM((GROUPS, 4 * CH, ROWS), BF16),
            pltpu.VMEM((GROUPS, ROWS, CH), BF16),
            pltpu.VMEM((CH // 2, 2 * FREQS, 2 * CH), BF16),
            pltpu.SemaphoreType.DMA((steps,)),
            pltpu.SemaphoreType.DMA((steps,)),
        ],
        compiler_params=pltpu.CompilerParams(vmem_limit_bytes=56 * 2**20),
        cost_estimate=pl.CostEstimate(flops=2**34, bytes_accessed=24 * 2**20, transcendentals=0),
        name="correlate_both" if signs == 2 else "correlate_one",
    )(own, partner, table)


def pick_kernel(index, source, out, held, in_sems, out_sems):
    blocks = range(held.shape[0])
    into = [
        pltpu.make_async_copy(source.at[index[c]], held.at[c], in_sems.at[c]) for c in blocks
    ]
    away = [pltpu.make_async_copy(held.at[c], out.at[c], out_sems.at[c]) for c in blocks]
    for copy in into:
        copy.start()
    for arrive, leave in zip(into, away):
        arrive.wait()
        leave.start()
    for copy in away:
        copy.wait()


def pick(source, index):
    return pl.pallas_call(
        pick_kernel,
        grid_spec=pltpu.PrefetchScalarGridSpec(
            num_scalar_prefetch=1,
            grid=(1,),
            in_specs=[pl.BlockSpec(memory_space=pltpu.HBM)],
            out_specs=pl.BlockSpec(memory_space=pltpu.HBM),
            scratch_shapes=[
                pltpu.VMEM(source.shape, source.dtype),
                pltpu.SemaphoreType.DMA((source.shape[0],)),
                pltpu.SemaphoreType.DMA((source.shape[0],)),
            ],
        ),
        out_shape=jax.ShapeDtypeStruct(source.shape, source.dtype),
        compiler_params=pltpu.CompilerParams(vmem_limit_bytes=58 * 2**20),
        cost_estimate=pl.CostEstimate(
            flops=0, bytes_accessed=2 * source.size * source.dtype.itemsize, transcendentals=0
        ),
        name="pick",
    )(index, source)


def at(values, index):
    hit = index[:, None] == jnp.arange(N_CHAN, dtype=jnp.int32)[None, :]
    return jnp.sum(jnp.where(hit, values[None, :], 0), axis=1)


def orient(pairing):
    zero, one = pairing[0], pairing[1]
    hop = at(one, zero)
    least = jnp.arange(N_CHAN, dtype=jnp.int32)
    for _ in range(3):
        least = jnp.minimum(least, at(least, hop))
        hop = at(hop, hop)
    handles_zero = least < at(least, zero)
    return handles_zero, jnp.where(handles_zero, zero, one), jnp.where(handles_zero, one, zero)


def over_chan(blocks):
    return lax.all_to_all(blocks, "chan", split_axis=0, concat_axis=0, tiled=True)


def sent_over_x(parts):
    got = [parts[0]]
    for shift in (2, 1, 3):
        route = [(x * 2 + y, (x + shift) % 4 * 2 + y) for x in range(4) for y in range(2)]
        got.append(lax.ppermute(parts[shift], "tm", route))
    return got


def sum_of(blocks):
    total = blocks[0].astype(F32)
    for block in blocks[1:]:
        total = total + block.astype(F32)
    return total


def sum_over_y(halves):
    mine = lax.axis_index("tm") % 2
    other = lax.dynamic_index_in_dim(halves, 1 - mine, 0, keepdims=False).astype(BF16)
    other = lax.ppermute(other, "tm", [(t, t ^ 1) for t in range(N_TM)])
    return lax.dynamic_index_in_dim(halves, mine, 0, keepdims=False) + other.astype(F32)


def body(traces, pairing):
    spec = whiten(traces)
    spread = over_chan(spec.reshape(N_CHAN, GROUPS // N_CHAN * ROWS, CH))
    own = expand(spec)
    handles_zero, handled, other = orient(pairing)
    table = jnp.asarray(np.concatenate([lag_rows()] * 2, axis=1))
    table = lax.dynamic_slice_in_dim(table, lax.axis_index("tm") // 2 * 32, 2 * LAGS, 1)
    spread, own, handled, other, table = lax.optimization_barrier(
        (spread, own, handled, other, table)
    )
    first = over_chan(pick(spread, handled)).reshape(GROUPS, ROWS, CH)
    second = over_chan(pick(spread, pairing[2])).reshape(GROUPS, ROWS, CH)
    pair_blocks = sent_over_x(correlate(own, first, table, 2))
    last_parts = correlate(own, second, table, 1)
    pair_blocks, last_parts = lax.optimization_barrier((pair_blocks, last_parts))
    pair_halves = sum_of(pair_blocks)
    last_blocks = sent_over_x(last_parts)
    behind = sum_over_y(pair_halves[:, 1])
    behind = over_chan(behind.reshape(N_CHAN, 64, CH).astype(BF16))
    behind = behind.at[other].get(mode="promise_in_bounds")
    last_blocks = lax.optimization_barrier((last_blocks, behind))[0]
    behind = over_chan(behind)
    ahead = sum_over_y(pair_halves[:, 0])
    last = sum_over_y(sum_of(last_blocks)[:, 0])

    def lags_first(value):
        return value.reshape(CH, 8, CH).transpose(1, 0, 2)

    forward = lags_first(ahead)
    backward = behind.astype(F32).reshape(CH, 8, CH).transpose(1, 2, 0)
    mine = lax.dynamic_index_in_dim(handles_zero, lax.axis_index("chan"), 0, keepdims=False)
    return jnp.stack(
        [
            jnp.where(mine, forward, backward),
            jnp.where(mine, backward, forward),
            lags_first(last),
        ]
    )


def solution(mesh):
    return jax.shard_map(
        body,
        mesh=mesh,
        in_specs=(P("chan", "tm", None), P()),
        out_specs=P(None, "tm", "chan", None),
        check_vma=False,
    )
```

```python
import functools
import math

import jax
import jax.numpy as jnp
import numpy as np
from jax import lax
from jax.experimental import pallas as pl
from jax.experimental.pallas import tpu as pltpu
from jax.sharding import PartitionSpec as P

FREQS = 256
SAMPLES = 512
LAGS = 64
CH = 128
WIN = 32
GROUPS = 64
ROWS = 256
N_CHAN = 16
N_TM = 8
WATER = 1.0
EPS = 1e-06
F32 = jnp.float32
BF16 = jnp.bfloat16


def forward_rows():
    freq = np.arange(FREQS)[:, None]
    sample = np.arange(SAMPLES)[None, :]
    phase = (freq * sample % SAMPLES) * (2.0 * math.pi / SAMPLES)
    both = np.stack([np.cos(phase), -np.sin(phase)], 0)
    both = both.reshape(2, GROUPS, 4, SAMPLES).transpose(1, 0, 2, 3)
    return both.reshape(2 * FREQS, SAMPLES).astype(np.float32).astype(BF16)


def lag_rows():
    lag = np.arange(LAGS)[:, None]
    freq = np.arange(FREQS)[None, :]
    phase = (lag * freq % SAMPLES) * (2.0 * math.pi / SAMPLES)
    both = np.stack([np.cos(phase), -np.sin(phase)], 0)
    both = both.reshape(2, N_TM, 1, 8, GROUPS, 1, 4)
    parity = np.eye(2).reshape(1, 1, 2, 1, 1, 2, 1)
    return (both * parity).reshape(2, 2 * LAGS, 2 * FREQS).astype(np.float32).astype(BF16)


def taper_row():
    pos = np.arange(SAMPLES)
    taper = 0.5 - 0.5 * np.cos((pos + 0.5) * (2.0 * math.pi / SAMPLES))
    return taper.astype(np.float32).reshape(1, SAMPLES)


CHUNK = 32
PITCH = 40
PART = 4


def whiten_kernel(
    traces, taper_hbm, table_hbm, out, raw, taper, table, tapered, white_rows, small_sems, in_sems, out_sems
):
    taper_copy = pltpu.make_async_copy(taper_hbm, taper, small_sems.at[0])
    table_copy = pltpu.make_async_copy(table_hbm, table, small_sems.at[1])

    def arrival(chunk):
        rows = pl.ds(chunk * CHUNK, CHUNK)
        return pltpu.make_async_copy(traces.at[rows], raw.at[rows], in_sems.at[chunk])

    def departure(part):
        rows = pl.ds(pl.multiple_of(part * PART * 16, PART * 16), PART * 16)
        return pltpu.make_async_copy(
            white_rows.at[:, rows, :], out.at[:, rows, :], out_sems.at[part]
        )

    taper_copy.start()
    for chunk in range(CH // CHUNK):
        arrival(chunk).start()
    table_copy.start()
    taper_copy.wait()

    def taper_step(chunk, carry):
        arrival(chunk).wait()
        for half in range(CHUNK // 8):
            first = chunk * CHUNK + half * 8
            rows = raw[pl.ds(first, 8)].astype(F32)
            rows = rows - jnp.mean(rows, axis=2, keepdims=True)
            rows = rows * taper[...].reshape(1, 1, SAMPLES)
            for inner in range(8):
                place = pl.ds((first + inner) * PITCH, WIN)
                for tile in range(4):
                    tapered[tile, place, :] = rows[inner, :, tile * 128 : tile * 128 + 128]
        return carry

    lax.fori_loop(0, CH // CHUNK, taper_step, 0)
    table_copy.wait()

    def window_pairs(part, carry):
        for pair in [part * PART + inner for inner in range(PART)]:
            columns = []
            for half in range(2):
                tiles = [
                    tapered[tile, pl.ds(pair * 2 + half, CH, stride=PITCH), :]
                    for tile in range(4)
                ]
                columns.append(jnp.concatenate(tiles, axis=1).astype(BF16))
            columns = jnp.concatenate(columns, axis=0)
            spec = lax.dot_general(
                table[...], columns, (((1,), (1,)), ((), ())), preferred_element_type=F32
            ).reshape(GROUPS, 8, 2 * CH)
            square = spec * spec
            level = jnp.sum(jnp.sum(square, axis=0), axis=0, keepdims=True) * (1.0 / FREQS)
            power = square + pltpu.roll(square, 4, 1)
            white = spec * lax.rsqrt(power + (WATER * level + EPS).reshape(1, 1, 2 * CH))
            white = jnp.concatenate([white[:, :, :CH], white[:, :, CH:]], axis=1)
            white_rows[:, pl.ds(pl.multiple_of(pair * 16, 16), 16), :] = white.astype(BF16)
        departure(part).start()
        return carry

    lax.fori_loop(0, WIN // 2 // PART, window_pairs, 0)
    for part in range(WIN // 2 // PART):
        departure(part).wait()


def whiten(traces):
    return pl.pallas_call(
        whiten_kernel,
        out_shape=jax.ShapeDtypeStruct((GROUPS, ROWS, CH), BF16),
        in_specs=[pl.BlockSpec(memory_space=pl.ANY)] * 3,
        out_specs=pl.BlockSpec(memory_space=pl.ANY),
        scratch_shapes=[
            pltpu.VMEM((CH, WIN, SAMPLES), BF16),
            pltpu.VMEM((1, SAMPLES), F32),
            pltpu.VMEM((2 * FREQS, SAMPLES), BF16),
            pltpu.VMEM((4, CH * PITCH, 128), F32),
            pltpu.VMEM((GROUPS, ROWS, CH), BF16),
            pltpu.SemaphoreType.DMA((2,)),
            pltpu.SemaphoreType.DMA((CH // CHUNK,)),
            pltpu.SemaphoreType.DMA((WIN // 2 // PART,)),
        ],
        compiler_params=pltpu.CompilerParams(vmem_limit_bytes=60 * 2**20),
        cost_estimate=pl.CostEstimate(flops=2 * 2**30, bytes_accessed=2**23, transcendentals=2**20),
        name="whiten",
    )(traces, jnp.asarray(taper_row()), jnp.asarray(forward_rows()))


def expand_kernel(spec, out, wide):
    lane = lax.broadcasted_iota(jnp.int32, (CH, ROWS), 1)
    for part in range(spec.shape[0]):
        turned = spec[part].astype(F32).T
        for f in range(4):
            kept = jnp.where(lane % 4 == f, turned, 0.0)
            for tile in range(2):
                wide[tile, pl.ds(f, CH, stride=4), :] = kept[:, tile * 128 : tile * 128 + 128]
        for tile in range(2):
            out[part, :, tile * 128 : tile * 128 + 128] = wide[tile].astype(BF16)


def expand(spec):
    per = 4
    return pl.pallas_call(
        expand_kernel,
        grid=(GROUPS // per,),
        out_shape=jax.ShapeDtypeStruct((GROUPS, 4 * CH, ROWS), BF16),
        in_specs=[pl.BlockSpec((per, ROWS, CH), lambda g: (g, 0, 0))],
        out_specs=pl.BlockSpec((per, 4 * CH, ROWS), lambda g: (g, 0, 0)),
        scratch_shapes=[pltpu.VMEM((2, 4 * CH, 128), F32)],
        compiler_params=pltpu.CompilerParams(vmem_limit_bytes=32 * 2**20),
        cost_estimate=pl.CostEstimate(flops=2**26, bytes_accessed=20 * 2**20, transcendentals=0),
        name="expand",
    )(spec)


def correlate_kernel(steps, own_hbm, partner_hbm, table, *refs):
    outs = refs[:4]
    own, partner, cross, own_sems, partner_sems = refs[4:]
    step = pl.program_id(0)
    per = GROUPS // steps
    sub = lax.broadcasted_iota(jnp.int32, (WIN, 8, CH), 1)

    def arrivals(chunk):
        groups = pl.ds(chunk * per, per)
        return (
            pltpu.make_async_copy(own_hbm.at[groups], own.at[groups], own_sems.at[chunk]),
            pltpu.make_async_copy(
                partner_hbm.at[groups], partner.at[groups], partner_sems.at[chunk]
            ),
        )

    @pl.when(step == 0)
    def _():
        for chunk in range(steps):
            for copy in arrivals(chunk):
                copy.start()

    @pl.when(step < steps)
    def _():
        for copy in arrivals(step):
            copy.wait()
        for pair in range(per // 2):
            halves = []
            for half in range(2):
                group = step * per + 2 * pair + half
                part = partner[group]
                wide = part.astype(F32).reshape(WIN, 8, CH)
                turned = jnp.where(sub < 4, -1.0, 1.0) * pltpu.roll(wide, 4, 1)
                right = jnp.concatenate([part, turned.reshape(ROWS, CH).astype(BF16)], axis=1)
                prod = jnp.dot(own[group], right, preferred_element_type=F32)
                halves.append(prod.reshape(CH // 2, 8, 2 * CH))
            rows = jnp.concatenate(halves, axis=1).astype(BF16)
            first = pl.multiple_of((step * (per // 2) + pair) * 16, 16)
            cross[:, pl.ds(first, 16), :] = rows

    @pl.when(step >= steps)
    def _():
        scale = 1.0 / math.sqrt(FREQS * WIN * N_TM)
        signs, chunk = outs[0].shape[1:3]
        base = (step - steps) * chunk

        def channel_pairs(idx, carry):
            first, second = cross[base + 2 * idx], cross[base + 2 * idx + 1]
            even = jnp.concatenate([first[:, :CH], second[:, :CH]], axis=1)
            odd = jnp.concatenate([first[:, CH:], second[:, CH:]], axis=1)
            even = jnp.dot(table[0], even, preferred_element_type=F32)
            odd = jnp.dot(table[1], odd, preferred_element_type=F32)
            for sign in range(signs):
                value = (even - odd if sign else even + odd) * scale
                value = value.astype(BF16).reshape(4, 2, 16, 2 * CH)
                for shift in range(4):
                    outs[shift][:, sign, 2 * idx] = value[shift, :, :, :CH]
                    outs[shift][:, sign, 2 * idx + 1] = value[shift, :, :, CH:]
            return carry

        lax.fori_loop(0, chunk // 2, channel_pairs, 0, unroll=8)


def correlate(own, partner, table, signs):
    per, chunk = 8, 16
    steps, late = GROUPS // per, CH // 2 // chunk
    block = pl.BlockSpec(
        (2, signs, chunk, 16, CH), lambda g: (0, 0, jnp.maximum(g - steps, 0), 0, 0)
    )
    return pl.pallas_call(
        functools.partial(correlate_kernel, steps),
        grid=(steps + late,),
        out_shape=[jax.ShapeDtypeStruct((2, signs, CH // 2, 16, CH), BF16)] * 4,
        in_specs=[
            pl.BlockSpec(memory_space=pl.ANY),
            pl.BlockSpec(memory_space=pl.ANY),
            pl.BlockSpec((2, 2 * LAGS, 2 * FREQS), lambda g: (0, 0, 0)),
        ],
        out_specs=[block] * 4,
        scratch_shapes=[
            pltpu.VMEM((GROUPS, 4 * CH, ROWS), BF16),
            pltpu.VMEM((GROUPS, ROWS, CH), BF16),
            pltpu.VMEM((CH // 2, 2 * FREQS, 2 * CH), BF16),
            pltpu.SemaphoreType.DMA((steps,)),
            pltpu.SemaphoreType.DMA((steps,)),
        ],
        compiler_params=pltpu.CompilerParams(vmem_limit_bytes=56 * 2**20),
        cost_estimate=pl.CostEstimate(flops=2**34, bytes_accessed=24 * 2**20, transcendentals=0),
        name="correlate_both" if signs == 2 else "correlate_one",
    )(own, partner, table)


def pick_kernel(index, source, out, held, in_sems, out_sems):
    blocks = range(held.shape[0])
    into = [
        pltpu.make_async_copy(source.at[index[c]], held.at[c], in_sems.at[c]) for c in blocks
    ]
    away = [pltpu.make_async_copy(held.at[c], out.at[c], out_sems.at[c]) for c in blocks]
    for copy in into:
        copy.start()
    for arrive, leave in zip(into, away):
        arrive.wait()
        leave.start()
    for copy in away:
        copy.wait()


def pick(source, index):
    return pl.pallas_call(
        pick_kernel,
        grid_spec=pltpu.PrefetchScalarGridSpec(
            num_scalar_prefetch=1,
            grid=(1,),
            in_specs=[pl.BlockSpec(memory_space=pltpu.HBM)],
            out_specs=pl.BlockSpec(memory_space=pltpu.HBM),
            scratch_shapes=[
                pltpu.VMEM(source.shape, source.dtype),
                pltpu.SemaphoreType.DMA((source.shape[0],)),
                pltpu.SemaphoreType.DMA((source.shape[0],)),
            ],
        ),
        out_shape=jax.ShapeDtypeStruct(source.shape, source.dtype),
        compiler_params=pltpu.CompilerParams(vmem_limit_bytes=58 * 2**20),
        cost_estimate=pl.CostEstimate(
            flops=0, bytes_accessed=2 * source.size * source.dtype.itemsize, transcendentals=0
        ),
        name="pick",
    )(index, source)


def at(values, index):
    hit = index[:, None] == jnp.arange(N_CHAN, dtype=jnp.int32)[None, :]
    return jnp.sum(jnp.where(hit, values[None, :], 0), axis=1)


def orient(pairing):
    zero, one = pairing[0], pairing[1]
    hop = at(one, zero)
    least = jnp.arange(N_CHAN, dtype=jnp.int32)
    for _ in range(3):
        least = jnp.minimum(least, at(least, hop))
        hop = at(hop, hop)
    handles_zero = least < at(least, zero)
    return handles_zero, jnp.where(handles_zero, zero, one), jnp.where(handles_zero, one, zero)


def over_chan(blocks):
    return lax.all_to_all(blocks, "chan", split_axis=0, concat_axis=0, tiled=True)


def sent_over_x(parts):
    got = [parts[0]]
    for shift in (2, 1, 3):
        route = [(x * 2 + y, (x + shift) % 4 * 2 + y) for x in range(4) for y in range(2)]
        got.append(lax.ppermute(parts[shift], "tm", route))
    return got


def sum_of(blocks):
    total = blocks[0].astype(F32)
    for block in blocks[1:]:
        total = total + block.astype(F32)
    return total


def sum_over_y(halves):
    mine = lax.axis_index("tm") % 2
    other = lax.dynamic_index_in_dim(halves, 1 - mine, 0, keepdims=False).astype(BF16)
    other = lax.ppermute(other, "tm", [(t, t ^ 1) for t in range(N_TM)])
    return lax.dynamic_index_in_dim(halves, mine, 0, keepdims=False) + other.astype(F32)


def body(traces, pairing):
    spec = whiten(traces)
    spread = over_chan(spec.reshape(N_CHAN, GROUPS // N_CHAN * ROWS, CH))
    own = expand(spec)
    handles_zero, handled, other = orient(pairing)
    table = jnp.asarray(np.concatenate([lag_rows()] * 2, axis=1))
    table = lax.dynamic_slice_in_dim(table, lax.axis_index("tm") // 2 * 32, 2 * LAGS, 1)
    spread, own, handled, other, table = lax.optimization_barrier(
        (spread, own, handled, other, table)
    )
    first = over_chan(pick(spread, handled)).reshape(GROUPS, ROWS, CH)
    second = over_chan(pick(spread, pairing[2])).reshape(GROUPS, ROWS, CH)
    pair_blocks = sent_over_x(correlate(own, first, table, 2))
    last_parts = correlate(own, second, table, 1)
    pair_blocks, last_parts = lax.optimization_barrier((pair_blocks, last_parts))
    pair_halves = sum_of(pair_blocks)
    last_blocks = sent_over_x(last_parts)
    behind = sum_over_y(pair_halves[:, 1])
    behind = over_chan(behind.reshape(N_CHAN, 64, CH).astype(BF16))
    behind = behind.at[other].get(mode="promise_in_bounds")
    last_blocks = lax.optimization_barrier((last_blocks, behind))[0]
    behind = over_chan(behind)
    ahead = sum_over_y(pair_halves[:, 0])
    last = sum_over_y(sum_of(last_blocks)[:, 0])

    def lags_first(value):
        return value.reshape(CH, 8, CH).transpose(1, 0, 2)

    forward = lags_first(ahead)
    backward = behind.astype(F32).reshape(CH, 8, CH).transpose(1, 2, 0)
    mine = lax.dynamic_index_in_dim(handles_zero, lax.axis_index("chan"), 0, keepdims=False)
    return jnp.stack(
        [
            jnp.where(mine, forward, backward),
            jnp.where(mine, backward, forward),
            lags_first(last),
        ]
    )


def solution(mesh):
    return jax.shard_map(
        body,
        mesh=mesh,
        in_specs=(P("chan", "tm", None), P()),
        out_specs=P(None, "tm", "chan", None),
        check_vma=False,
    )
```

```python
import functools
import math

import jax
import jax.numpy as jnp
import numpy as np
from jax import lax
from jax.experimental import pallas as pl
from jax.experimental.pallas import tpu as pltpu
from jax.sharding import PartitionSpec as P

FREQS = 256
SAMPLES = 512
LAGS = 64
CH = 128
WIN = 32
GROUPS = 64
ROWS = 256
N_CHAN = 16
N_TM = 8
WATER = 1.0
EPS = 1e-06
F32 = jnp.float32
BF16 = jnp.bfloat16


def forward_rows():
    freq = np.arange(FREQS)[:, None]
    sample = np.arange(SAMPLES)[None, :]
    phase = (freq * sample % SAMPLES) * (2.0 * math.pi / SAMPLES)
    both = np.stack([np.cos(phase), -np.sin(phase)], 0)
    both = both.reshape(2, GROUPS, 4, SAMPLES).transpose(1, 0, 2, 3)
    return both.reshape(2 * FREQS, SAMPLES).astype(np.float32).astype(BF16)


def lag_rows():
    lag = np.arange(LAGS)[:, None]
    freq = np.arange(FREQS)[None, :]
    phase = (lag * freq % SAMPLES) * (2.0 * math.pi / SAMPLES)
    both = np.stack([np.cos(phase), -np.sin(phase)], 0)
    both = both.reshape(2, N_TM, 1, 8, GROUPS, 1, 4)
    parity = np.eye(2).reshape(1, 1, 2, 1, 1, 2, 1)
    return (both * parity).reshape(2, 2 * LAGS, 2 * FREQS).astype(np.float32).astype(BF16)


def taper_row():
    pos = np.arange(SAMPLES)
    taper = 0.5 - 0.5 * np.cos((pos + 0.5) * (2.0 * math.pi / SAMPLES))
    return taper.astype(np.float32).reshape(1, SAMPLES)


CHUNK = 32
PITCH = 40
PART = 4


def whiten_kernel(
    traces, taper_hbm, table_hbm, out, raw, taper, table, tapered, white_rows, small_sems, in_sems, out_sems
):
    taper_copy = pltpu.make_async_copy(taper_hbm, taper, small_sems.at[0])
    table_copy = pltpu.make_async_copy(table_hbm, table, small_sems.at[1])

    def arrival(chunk):
        rows = pl.ds(chunk * CHUNK, CHUNK)
        return pltpu.make_async_copy(traces.at[rows], raw.at[rows], in_sems.at[chunk])

    def departure(part):
        rows = pl.ds(pl.multiple_of(part * PART * 16, PART * 16), PART * 16)
        return pltpu.make_async_copy(
            white_rows.at[:, rows, :], out.at[:, rows, :], out_sems.at[part]
        )

    taper_copy.start()
    for chunk in range(CH // CHUNK):
        arrival(chunk).start()
    table_copy.start()
    taper_copy.wait()

    def taper_step(chunk, carry):
        arrival(chunk).wait()
        for half in range(CHUNK // 8):
            first = chunk * CHUNK + half * 8
            rows = raw[pl.ds(first, 8)].astype(F32)
            rows = rows - jnp.mean(rows, axis=2, keepdims=True)
            rows = rows * taper[...].reshape(1, 1, SAMPLES)
            for inner in range(8):
                place = pl.ds((first + inner) * PITCH, WIN)
                for tile in range(4):
                    tapered[tile, place, :] = rows[inner, :, tile * 128 : tile * 128 + 128]
        return carry

    lax.fori_loop(0, CH // CHUNK, taper_step, 0)
    table_copy.wait()

    def window_pairs(part, carry):
        for pair in [part * PART + inner for inner in range(PART)]:
            columns = []
            for half in range(2):
                tiles = [
                    tapered[tile, pl.ds(pair * 2 + half, CH, stride=PITCH), :]
                    for tile in range(4)
                ]
                columns.append(jnp.concatenate(tiles, axis=1).astype(BF16))
            columns = jnp.concatenate(columns, axis=0)
            spec = lax.dot_general(
                table[...], columns, (((1,), (1,)), ((), ())), preferred_element_type=F32
            ).reshape(GROUPS, 8, 2 * CH)
            square = spec * spec
            level = jnp.sum(jnp.sum(square, axis=0), axis=0, keepdims=True) * (1.0 / FREQS)
            power = square + pltpu.roll(square, 4, 1)
            white = spec * lax.rsqrt(power + (WATER * level + EPS).reshape(1, 1, 2 * CH))
            white = jnp.concatenate([white[:, :, :CH], white[:, :, CH:]], axis=1)
            white_rows[:, pl.ds(pl.multiple_of(pair * 16, 16), 16), :] = white.astype(BF16)
        departure(part).start()
        return carry

    lax.fori_loop(0, WIN // 2 // PART, window_pairs, 0)
    for part in range(WIN // 2 // PART):
        departure(part).wait()


def whiten(traces):
    return pl.pallas_call(
        whiten_kernel,
        out_shape=jax.ShapeDtypeStruct((GROUPS, ROWS, CH), BF16),
        in_specs=[pl.BlockSpec(memory_space=pl.ANY)] * 3,
        out_specs=pl.BlockSpec(memory_space=pl.ANY),
        scratch_shapes=[
            pltpu.VMEM((CH, WIN, SAMPLES), BF16),
            pltpu.VMEM((1, SAMPLES), F32),
            pltpu.VMEM((2 * FREQS, SAMPLES), BF16),
            pltpu.VMEM((4, CH * PITCH, 128), F32),
            pltpu.VMEM((GROUPS, ROWS, CH), BF16),
            pltpu.SemaphoreType.DMA((2,)),
            pltpu.SemaphoreType.DMA((CH // CHUNK,)),
            pltpu.SemaphoreType.DMA((WIN // 2 // PART,)),
        ],
        compiler_params=pltpu.CompilerParams(vmem_limit_bytes=60 * 2**20),
        cost_estimate=pl.CostEstimate(flops=2 * 2**30, bytes_accessed=2**23, transcendentals=2**20),
        name="whiten",
    )(traces, jnp.asarray(taper_row()), jnp.asarray(forward_rows()))


def expand_kernel(spec, out, wide):
    lane = lax.broadcasted_iota(jnp.int32, (CH, ROWS), 1)
    for part in range(spec.shape[0]):
        turned = spec[part].astype(F32).T
        for f in range(4):
            kept = jnp.where(lane % 4 == f, turned, 0.0)
            for tile in range(2):
                wide[tile, pl.ds(f, CH, stride=4), :] = kept[:, tile * 128 : tile * 128 + 128]
        for tile in range(2):
            out[part, :, tile * 128 : tile * 128 + 128] = wide[tile].astype(BF16)


def expand(spec):
    per = 4
    return pl.pallas_call(
        expand_kernel,
        grid=(GROUPS // per,),
        out_shape=jax.ShapeDtypeStruct((GROUPS, 4 * CH, ROWS), BF16),
        in_specs=[pl.BlockSpec((per, ROWS, CH), lambda g: (g, 0, 0))],
        out_specs=pl.BlockSpec((per, 4 * CH, ROWS), lambda g: (g, 0, 0)),
        scratch_shapes=[pltpu.VMEM((2, 4 * CH, 128), F32)],
        compiler_params=pltpu.CompilerParams(vmem_limit_bytes=32 * 2**20),
        cost_estimate=pl.CostEstimate(flops=2**26, bytes_accessed=20 * 2**20, transcendentals=0),
        name="expand",
    )(spec)


def correlate_kernel(steps, own_hbm, partner_hbm, table, *refs):
    outs = refs[:-5]
    own, partner, cross, own_sems, partner_sems = refs[-5:]
    step = pl.program_id(0)
    per = GROUPS // steps
    sub = lax.broadcasted_iota(jnp.int32, (WIN, 8, CH), 1)

    def arrivals(chunk):
        groups = pl.ds(chunk * per, per)
        return (
            pltpu.make_async_copy(own_hbm.at[groups], own.at[groups], own_sems.at[chunk]),
            pltpu.make_async_copy(
                partner_hbm.at[groups], partner.at[groups], partner_sems.at[chunk]
            ),
        )

    @pl.when(step == 0)
    def _():
        for chunk in range(steps):
            for copy in arrivals(chunk):
                copy.start()

    @pl.when(step < steps)
    def _():
        for copy in arrivals(step):
            copy.wait()
        for pair in range(per // 2):
            halves = []
            for half in range(2):
                group = step * per + 2 * pair + half
                part = partner[group]
                wide = part.astype(F32).reshape(WIN, 8, CH)
                turned = jnp.where(sub < 4, -1.0, 1.0) * pltpu.roll(wide, 4, 1)
                right = jnp.concatenate([part, turned.reshape(ROWS, CH).astype(BF16)], axis=1)
                prod = jnp.dot(own[group], right, preferred_element_type=F32)
                halves.append(prod.reshape(CH // 2, 8, 2 * CH))
            rows = jnp.concatenate(halves, axis=1).astype(BF16)
            first = pl.multiple_of((step * (per // 2) + pair) * 16, 16)
            cross[:, pl.ds(first, 16), :] = rows

    @pl.when(step >= steps)
    def _():
        scale = 1.0 / math.sqrt(FREQS * WIN * N_TM)
        chunk = outs[0].shape[1]
        base = (step - steps) * chunk

        def channel_pairs(idx, carry):
            first, second = cross[base + 2 * idx], cross[base + 2 * idx + 1]
            even = jnp.concatenate([first[:, :CH], second[:, :CH]], axis=1)
            odd = jnp.concatenate([first[:, CH:], second[:, CH:]], axis=1)
            even = jnp.dot(table[0], even, preferred_element_type=F32)
            odd = jnp.dot(table[1], odd, preferred_element_type=F32)
            for sign in range(len(outs) // 4):
                value = (even - odd if sign else even + odd) * scale
                value = value.astype(BF16).reshape(4, 2, 16, 2 * CH)
                for shift in range(4):
                    outs[4 * sign + shift][:, 2 * idx] = value[shift, :, :, :CH]
                    outs[4 * sign + shift][:, 2 * idx + 1] = value[shift, :, :, CH:]
            return carry

        lax.fori_loop(0, chunk // 2, channel_pairs, 0, unroll=8)


def correlate(own, partner, table, signs):
    per, chunk = 8, 16
    steps, late = GROUPS // per, CH // 2 // chunk
    block = pl.BlockSpec((2, chunk, 16, CH), lambda g: (0, jnp.maximum(g - steps, 0), 0, 0))
    return pl.pallas_call(
        functools.partial(correlate_kernel, steps),
        grid=(steps + late,),
        out_shape=[jax.ShapeDtypeStruct((2, CH // 2, 16, CH), BF16)] * (4 * signs),
        in_specs=[
            pl.BlockSpec(memory_space=pl.ANY),
            pl.BlockSpec(memory_space=pl.ANY),
            pl.BlockSpec((2, 2 * LAGS, 2 * FREQS), lambda g: (0, 0, 0)),
        ],
        out_specs=[block] * (4 * signs),
        scratch_shapes=[
            pltpu.VMEM((GROUPS, 4 * CH, ROWS), BF16),
            pltpu.VMEM((GROUPS, ROWS, CH), BF16),
            pltpu.VMEM((CH // 2, 2 * FREQS, 2 * CH), BF16),
            pltpu.SemaphoreType.DMA((steps,)),
            pltpu.SemaphoreType.DMA((steps,)),
        ],
        compiler_params=pltpu.CompilerParams(vmem_limit_bytes=56 * 2**20),
        cost_estimate=pl.CostEstimate(flops=2**34, bytes_accessed=24 * 2**20, transcendentals=0),
        name="correlate_both" if signs == 2 else "correlate_one",
    )(own, partner, table)


def pick_kernel(index, source, out, held, in_sems, out_sems):
    blocks = range(held.shape[0])
    into = [
        pltpu.make_async_copy(source.at[index[c]], held.at[c], in_sems.at[c]) for c in blocks
    ]
    away = [pltpu.make_async_copy(held.at[c], out.at[c], out_sems.at[c]) for c in blocks]
    for copy in into:
        copy.start()
    for arrive, leave in zip(into, away):
        arrive.wait()
        leave.start()
    for copy in away:
        copy.wait()


def pick(source, index):
    return pl.pallas_call(
        pick_kernel,
        grid_spec=pltpu.PrefetchScalarGridSpec(
            num_scalar_prefetch=1,
            grid=(1,),
            in_specs=[pl.BlockSpec(memory_space=pltpu.HBM)],
            out_specs=pl.BlockSpec(memory_space=pltpu.HBM),
            scratch_shapes=[
                pltpu.VMEM(source.shape, source.dtype),
                pltpu.SemaphoreType.DMA((source.shape[0],)),
                pltpu.SemaphoreType.DMA((source.shape[0],)),
            ],
        ),
        out_shape=jax.ShapeDtypeStruct(source.shape, source.dtype),
        compiler_params=pltpu.CompilerParams(vmem_limit_bytes=58 * 2**20),
        cost_estimate=pl.CostEstimate(
            flops=0, bytes_accessed=2 * source.size * source.dtype.itemsize, transcendentals=0
        ),
        name="pick",
    )(index, source)


def at(values, index):
    hit = index[:, None] == jnp.arange(N_CHAN, dtype=jnp.int32)[None, :]
    return jnp.sum(jnp.where(hit, values[None, :], 0), axis=1)


def orient(pairing):
    zero, one = pairing[0], pairing[1]
    hop = at(one, zero)
    least = jnp.arange(N_CHAN, dtype=jnp.int32)
    for _ in range(3):
        least = jnp.minimum(least, at(least, hop))
        hop = at(hop, hop)
    handles_zero = least < at(least, zero)
    return handles_zero, jnp.where(handles_zero, zero, one), jnp.where(handles_zero, one, zero)


def over_chan(blocks):
    return lax.all_to_all(blocks, "chan", split_axis=0, concat_axis=0, tiled=True)


def sent_over_x(parts):
    got = [parts[0]]
    for shift in (2, 1, 3):
        route = [(x * 2 + y, (x + shift) % 4 * 2 + y) for x in range(4) for y in range(2)]
        got.append(lax.ppermute(parts[shift], "tm", route))
    return got


def sum_of(blocks):
    total = blocks[0].astype(F32)
    for block in blocks[1:]:
        total = total + block.astype(F32)
    return total


def sum_over_y(halves):
    mine = lax.axis_index("tm") % 2
    other = lax.dynamic_index_in_dim(halves, 1 - mine, 0, keepdims=False).astype(BF16)
    other = lax.ppermute(other, "tm", [(t, t ^ 1) for t in range(N_TM)])
    return lax.dynamic_index_in_dim(halves, mine, 0, keepdims=False) + other.astype(F32)


def body(traces, pairing):
    spec = whiten(traces)
    spread = over_chan(spec.reshape(N_CHAN, GROUPS // N_CHAN * ROWS, CH))
    own = expand(spec)
    handles_zero, handled, other = orient(pairing)
    table = jnp.asarray(np.concatenate([lag_rows()] * 2, axis=1))
    table = lax.dynamic_slice_in_dim(table, lax.axis_index("tm") // 2 * 32, 2 * LAGS, 1)
    spread, own, handled, other, table = lax.optimization_barrier(
        (spread, own, handled, other, table)
    )
    first = over_chan(pick(spread, handled)).reshape(GROUPS, ROWS, CH)
    second = over_chan(pick(spread, pairing[2])).reshape(GROUPS, ROWS, CH)
    pair_parts = correlate(own, first, table, 2)
    behind = sent_over_x(pair_parts[4:])
    behind, pair_parts = lax.optimization_barrier((behind, pair_parts[:4]))
    pair_blocks = sent_over_x(pair_parts)
    behind = sum_over_y(sum_of(behind)).reshape(N_CHAN, 64, CH).astype(BF16)
    behind, second = lax.optimization_barrier((behind, second))
    last_parts = correlate(own, second, table, 1)
    behind = over_chan(behind)
    behind, pair_blocks, last_parts = lax.optimization_barrier((behind, pair_blocks, last_parts))
    last_blocks = sent_over_x(last_parts)
    behind = behind.at[other].get(mode="promise_in_bounds")
    last_blocks = lax.optimization_barrier((last_blocks, behind))[0]
    behind = over_chan(behind)
    ahead = sum_over_y(sum_of(pair_blocks))
    last = sum_over_y(sum_of(last_blocks))

    def lags_first(value):
        return value.reshape(CH, 8, CH).transpose(1, 0, 2)

    forward = lags_first(ahead)
    backward = behind.astype(F32).reshape(CH, 8, CH).transpose(1, 2, 0)
    mine = lax.dynamic_index_in_dim(handles_zero, lax.axis_index("chan"), 0, keepdims=False)
    return jnp.stack(
        [
            jnp.where(mine, forward, backward),
            jnp.where(mine, backward, forward),
            lags_first(last),
        ]
    )


def solution(mesh):
    return jax.shard_map(
        body,
        mesh=mesh,
        in_specs=(P("chan", "tm", None), P()),
        out_specs=P(None, "tm", "chan", None),
        check_vma=False,
    )
```

```python
import functools
import math

import jax
import jax.numpy as jnp
import numpy as np
from jax import lax
from jax.experimental import pallas as pl
from jax.experimental.pallas import tpu as pltpu
from jax.sharding import PartitionSpec as P

FREQS = 256
SAMPLES = 512
LAGS = 64
CH = 128
WIN = 32
GROUPS = 64
ROWS = 256
N_CHAN = 16
N_TM = 8
WATER = 1.0
EPS = 1e-06
F32 = jnp.float32
BF16 = jnp.bfloat16


def forward_rows():
    freq = np.arange(FREQS)[:, None]
    sample = np.arange(SAMPLES)[None, :]
    phase = (freq * sample % SAMPLES) * (2.0 * math.pi / SAMPLES)
    both = np.stack([np.cos(phase), -np.sin(phase)], 0)
    both = both.reshape(2, GROUPS, 4, SAMPLES).transpose(1, 0, 2, 3)
    return both.reshape(2 * FREQS, SAMPLES).astype(np.float32).astype(BF16)


def lag_rows():
    lag = np.arange(LAGS)[:, None]
    freq = np.arange(FREQS)[None, :]
    phase = (lag * freq % SAMPLES) * (2.0 * math.pi / SAMPLES)
    both = np.stack([np.cos(phase), -np.sin(phase)], 0)
    both = both.reshape(2, N_TM, 1, 8, GROUPS, 1, 4)
    parity = np.eye(2).reshape(1, 1, 2, 1, 1, 2, 1)
    return (both * parity).reshape(2, 2 * LAGS, 2 * FREQS).astype(np.float32).astype(BF16)


def taper_row():
    pos = np.arange(SAMPLES)
    taper = 0.5 - 0.5 * np.cos((pos + 0.5) * (2.0 * math.pi / SAMPLES))
    return taper.astype(np.float32).reshape(1, SAMPLES)


CHUNK = 32
PITCH = 40
PART = 4


def whiten_kernel(
    traces, taper_hbm, table_hbm, out, raw, taper, table, tapered, white_rows, small_sems, in_sems, out_sems
):
    taper_copy = pltpu.make_async_copy(taper_hbm, taper, small_sems.at[0])
    table_copy = pltpu.make_async_copy(table_hbm, table, small_sems.at[1])

    def arrival(chunk):
        rows = pl.ds(chunk * CHUNK, CHUNK)
        return pltpu.make_async_copy(traces.at[rows], raw.at[rows], in_sems.at[chunk])

    def departure(part):
        rows = pl.ds(pl.multiple_of(part * PART * 16, PART * 16), PART * 16)
        return pltpu.make_async_copy(
            white_rows.at[:, rows, :], out.at[:, rows, :], out_sems.at[part]
        )

    taper_copy.start()
    for chunk in range(CH // CHUNK):
        arrival(chunk).start()
    table_copy.start()
    taper_copy.wait()

    def taper_step(chunk, carry):
        arrival(chunk).wait()
        for half in range(CHUNK // 8):
            first = chunk * CHUNK + half * 8
            rows = raw[pl.ds(first, 8)].astype(F32)
            rows = rows - jnp.mean(rows, axis=2, keepdims=True)
            rows = rows * taper[...].reshape(1, 1, SAMPLES)
            for inner in range(8):
                place = pl.ds((first + inner) * PITCH, WIN)
                for tile in range(4):
                    tapered[tile, place, :] = rows[inner, :, tile * 128 : tile * 128 + 128]
        return carry

    lax.fori_loop(0, CH // CHUNK, taper_step, 0)
    table_copy.wait()

    def window_pairs(part, carry):
        for pair in [part * PART + inner for inner in range(PART)]:
            columns = []
            for half in range(2):
                tiles = [
                    tapered[tile, pl.ds(pair * 2 + half, CH, stride=PITCH), :]
                    for tile in range(4)
                ]
                columns.append(jnp.concatenate(tiles, axis=1).astype(BF16))
            columns = jnp.concatenate(columns, axis=0)
            spec = lax.dot_general(
                table[...], columns, (((1,), (1,)), ((), ())), preferred_element_type=F32
            ).reshape(GROUPS, 8, 2 * CH)
            square = spec * spec
            level = jnp.sum(jnp.sum(square, axis=0), axis=0, keepdims=True) * (1.0 / FREQS)
            power = square + pltpu.roll(square, 4, 1)
            white = spec * lax.rsqrt(power + (WATER * level + EPS).reshape(1, 1, 2 * CH))
            white = jnp.concatenate([white[:, :, :CH], white[:, :, CH:]], axis=1)
            white_rows[:, pl.ds(pl.multiple_of(pair * 16, 16), 16), :] = white.astype(BF16)
        departure(part).start()
        return carry

    lax.fori_loop(0, WIN // 2 // PART, window_pairs, 0)
    for part in range(WIN // 2 // PART):
        departure(part).wait()


def whiten(traces):
    return pl.pallas_call(
        whiten_kernel,
        out_shape=jax.ShapeDtypeStruct((GROUPS, ROWS, CH), BF16),
        in_specs=[pl.BlockSpec(memory_space=pl.ANY)] * 3,
        out_specs=pl.BlockSpec(memory_space=pl.ANY),
        scratch_shapes=[
            pltpu.VMEM((CH, WIN, SAMPLES), BF16),
            pltpu.VMEM((1, SAMPLES), F32),
            pltpu.VMEM((2 * FREQS, SAMPLES), BF16),
            pltpu.VMEM((4, CH * PITCH, 128), F32),
            pltpu.VMEM((GROUPS, ROWS, CH), BF16),
            pltpu.SemaphoreType.DMA((2,)),
            pltpu.SemaphoreType.DMA((CH // CHUNK,)),
            pltpu.SemaphoreType.DMA((WIN // 2 // PART,)),
        ],
        compiler_params=pltpu.CompilerParams(vmem_limit_bytes=60 * 2**20),
        cost_estimate=pl.CostEstimate(flops=2 * 2**30, bytes_accessed=2**23, transcendentals=2**20),
        name="whiten",
    )(traces, jnp.asarray(taper_row()), jnp.asarray(forward_rows()))


def expand_kernel(spec, out, wide):
    lane = lax.broadcasted_iota(jnp.int32, (CH, ROWS), 1)
    for part in range(spec.shape[0]):
        turned = spec[part].astype(F32).T
        for f in range(4):
            kept = jnp.where(lane % 4 == f, turned, 0.0)
            for tile in range(2):
                wide[tile, pl.ds(f, CH, stride=4), :] = kept[:, tile * 128 : tile * 128 + 128]
        for tile in range(2):
            out[part, :, tile * 128 : tile * 128 + 128] = wide[tile].astype(BF16)


def expand(spec):
    per = 4
    return pl.pallas_call(
        expand_kernel,
        grid=(GROUPS // per,),
        out_shape=jax.ShapeDtypeStruct((GROUPS, 4 * CH, ROWS), BF16),
        in_specs=[pl.BlockSpec((per, ROWS, CH), lambda g: (g, 0, 0))],
        out_specs=pl.BlockSpec((per, 4 * CH, ROWS), lambda g: (g, 0, 0)),
        scratch_shapes=[pltpu.VMEM((2, 4 * CH, 128), F32)],
        compiler_params=pltpu.CompilerParams(vmem_limit_bytes=32 * 2**20),
        cost_estimate=pl.CostEstimate(flops=2**26, bytes_accessed=20 * 2**20, transcendentals=0),
        name="expand",
    )(spec)


def correlate_kernel(steps, own_hbm, partner_hbm, table, *refs):
    outs = refs[:-5]
    own, partner, cross, own_sems, partner_sems = refs[-5:]
    step = pl.program_id(0)
    per = GROUPS // steps
    sub = lax.broadcasted_iota(jnp.int32, (WIN, 8, CH), 1)

    def arrivals(chunk):
        groups = pl.ds(chunk * per, per)
        return (
            pltpu.make_async_copy(own_hbm.at[groups], own.at[groups], own_sems.at[chunk]),
            pltpu.make_async_copy(
                partner_hbm.at[groups], partner.at[groups], partner_sems.at[chunk]
            ),
        )

    @pl.when(step == 0)
    def _():
        for chunk in range(steps):
            for copy in arrivals(chunk):
                copy.start()

    @pl.when(step < steps)
    def _():
        for copy in arrivals(step):
            copy.wait()
        for pair in range(per // 2):
            halves = []
            for half in range(2):
                group = step * per + 2 * pair + half
                part = partner[group]
                wide = part.astype(F32).reshape(WIN, 8, CH)
                turned = jnp.where(sub < 4, -1.0, 1.0) * pltpu.roll(wide, 4, 1)
                right = jnp.concatenate([part, turned.reshape(ROWS, CH).astype(BF16)], axis=1)
                prod = jnp.dot(own[group], right, preferred_element_type=F32)
                halves.append(prod.reshape(CH // 2, 8, 2 * CH))
            rows = jnp.concatenate(halves, axis=1).astype(BF16)
            first = pl.multiple_of((step * (per // 2) + pair) * 16, 16)
            cross[:, pl.ds(first, 16), :] = rows

    @pl.when(step >= steps)
    def _():
        scale = 1.0 / math.sqrt(FREQS * WIN * N_TM)
        chunk = outs[0].shape[1]
        base = (step - steps) * chunk

        def channel_pairs(idx, carry):
            first, second = cross[base + 2 * idx], cross[base + 2 * idx + 1]
            even = jnp.concatenate([first[:, :CH], second[:, :CH]], axis=1)
            odd = jnp.concatenate([first[:, CH:], second[:, CH:]], axis=1)
            even = jnp.dot(table[0], even, preferred_element_type=F32)
            odd = jnp.dot(table[1], odd, preferred_element_type=F32)
            for sign in range(len(outs) // 4):
                value = (even - odd if sign else even + odd) * scale
                value = value.astype(BF16).reshape(4, 2, 16, 2 * CH)
                for shift in range(4):
                    outs[4 * sign + shift][:, 2 * idx] = value[shift, :, :, :CH]
                    outs[4 * sign + shift][:, 2 * idx + 1] = value[shift, :, :, CH:]
            return carry

        lax.fori_loop(0, chunk // 2, channel_pairs, 0, unroll=8)


def correlate(own, partner, table, signs):
    per, chunk = 8, 16
    steps, late = GROUPS // per, CH // 2 // chunk
    block = pl.BlockSpec((2, chunk, 16, CH), lambda g: (0, jnp.maximum(g - steps, 0), 0, 0))
    return pl.pallas_call(
        functools.partial(correlate_kernel, steps),
        grid=(steps + late,),
        out_shape=[jax.ShapeDtypeStruct((2, CH // 2, 16, CH), BF16)] * (4 * signs),
        in_specs=[
            pl.BlockSpec(memory_space=pl.ANY),
            pl.BlockSpec(memory_space=pl.ANY),
            pl.BlockSpec((2, 2 * LAGS, 2 * FREQS), lambda g: (0, 0, 0)),
        ],
        out_specs=[block] * (4 * signs),
        scratch_shapes=[
            pltpu.VMEM((GROUPS, 4 * CH, ROWS), BF16),
            pltpu.VMEM((GROUPS, ROWS, CH), BF16),
            pltpu.VMEM((CH // 2, 2 * FREQS, 2 * CH), BF16),
            pltpu.SemaphoreType.DMA((steps,)),
            pltpu.SemaphoreType.DMA((steps,)),
        ],
        compiler_params=pltpu.CompilerParams(vmem_limit_bytes=56 * 2**20),
        cost_estimate=pl.CostEstimate(flops=2**34, bytes_accessed=24 * 2**20, transcendentals=0),
        name="correlate_both" if signs == 2 else "correlate_one",
    )(own, partner, table)


def pick_kernel(index, source, out, held, in_sems, out_sems):
    blocks = range(held.shape[0])
    into = [
        pltpu.make_async_copy(source.at[index[c]], held.at[c], in_sems.at[c]) for c in blocks
    ]
    away = [pltpu.make_async_copy(held.at[c], out.at[c], out_sems.at[c]) for c in blocks]
    for copy in into:
        copy.start()
    for arrive, leave in zip(into, away):
        arrive.wait()
        leave.start()
    for copy in away:
        copy.wait()


def pick(source, index):
    return pl.pallas_call(
        pick_kernel,
        grid_spec=pltpu.PrefetchScalarGridSpec(
            num_scalar_prefetch=1,
            grid=(1,),
            in_specs=[pl.BlockSpec(memory_space=pltpu.HBM)],
            out_specs=pl.BlockSpec(memory_space=pltpu.HBM),
            scratch_shapes=[
                pltpu.VMEM(source.shape, source.dtype),
                pltpu.SemaphoreType.DMA((source.shape[0],)),
                pltpu.SemaphoreType.DMA((source.shape[0],)),
            ],
        ),
        out_shape=jax.ShapeDtypeStruct(source.shape, source.dtype),
        compiler_params=pltpu.CompilerParams(vmem_limit_bytes=58 * 2**20),
        cost_estimate=pl.CostEstimate(
            flops=0, bytes_accessed=2 * source.size * source.dtype.itemsize, transcendentals=0
        ),
        name="pick",
    )(index, source)


def at(values, index):
    hit = index[:, None] == jnp.arange(N_CHAN, dtype=jnp.int32)[None, :]
    return jnp.sum(jnp.where(hit, values[None, :], 0), axis=1)


def orient(pairing):
    zero, one = pairing[0], pairing[1]
    hop = at(one, zero)
    least = jnp.arange(N_CHAN, dtype=jnp.int32)
    for _ in range(3):
        least = jnp.minimum(least, at(least, hop))
        hop = at(hop, hop)
    handles_zero = least < at(least, zero)
    return handles_zero, jnp.where(handles_zero, zero, one), jnp.where(handles_zero, one, zero)


def over_chan(blocks):
    return lax.all_to_all(blocks, "chan", split_axis=0, concat_axis=0, tiled=True)


def sent_over_x(parts):
    got = [parts[0]]
    for shift in (2, 1, 3):
        route = [(x * 2 + y, (x + shift) % 4 * 2 + y) for x in range(4) for y in range(2)]
        got.append(lax.ppermute(parts[shift], "tm", route))
    return got


def sum_of(blocks):
    total = blocks[0].astype(F32)
    for block in blocks[1:]:
        total = total + block.astype(F32)
    return total


def sum_over_y(halves):
    mine = lax.axis_index("tm") % 2
    other = lax.dynamic_index_in_dim(halves, 1 - mine, 0, keepdims=False).astype(BF16)
    other = lax.ppermute(other, "tm", [(t, t ^ 1) for t in range(N_TM)])
    return lax.dynamic_index_in_dim(halves, mine, 0, keepdims=False) + other.astype(F32)


def body(traces, pairing):
    spec = whiten(traces)
    spread = over_chan(spec.reshape(N_CHAN, GROUPS // N_CHAN * ROWS, CH))
    own = expand(spec)
    handles_zero, handled, other = orient(pairing)
    table = jnp.asarray(np.concatenate([lag_rows()] * 2, axis=1))
    table = lax.dynamic_slice_in_dim(table, lax.axis_index("tm") // 2 * 32, 2 * LAGS, 1)
    spread, own, handled, other, table = lax.optimization_barrier(
        (spread, own, handled, other, table)
    )
    first = over_chan(pick(spread, handled)).reshape(GROUPS, ROWS, CH)
    second = over_chan(pick(spread, pairing[2])).reshape(GROUPS, ROWS, CH)
    pair_parts = correlate(own, first, table, 2)
    behind = sum_over_y(sum_of(sent_over_x(pair_parts[4:])))
    pair_blocks = sent_over_x(pair_parts[:4])
    last_parts = correlate(own, second, table, 1)
    behind, pair_blocks, last_parts = lax.optimization_barrier((behind, pair_blocks, last_parts))
    behind = over_chan(behind.reshape(N_CHAN, 64, CH).astype(BF16))
    last_blocks = sent_over_x(last_parts)
    behind = behind.at[other].get(mode="promise_in_bounds")
    last_blocks = lax.optimization_barrier((last_blocks, behind))[0]
    behind = over_chan(behind)
    ahead = sum_over_y(sum_of(pair_blocks))
    last = sum_over_y(sum_of(last_blocks))

    def lags_first(value):
        return value.reshape(CH, 8, CH).transpose(1, 0, 2)

    forward = lags_first(ahead)
    backward = behind.astype(F32).reshape(CH, 8, CH).transpose(1, 2, 0)
    mine = lax.dynamic_index_in_dim(handles_zero, lax.axis_index("chan"), 0, keepdims=False)
    return jnp.stack(
        [
            jnp.where(mine, forward, backward),
            jnp.where(mine, backward, forward),
            lags_first(last),
        ]
    )


def solution(mesh):
    return jax.shard_map(
        body,
        mesh=mesh,
        in_specs=(P("chan", "tm", None), P()),
        out_specs=P(None, "tm", "chan", None),
        check_vma=False,
    )
```

```python
import functools
import math

import jax
import jax.numpy as jnp
import numpy as np
from jax import lax
from jax.experimental import pallas as pl
from jax.experimental.pallas import tpu as pltpu
from jax.sharding import PartitionSpec as P

FREQS = 256
SAMPLES = 512
LAGS = 64
CH = 128
WIN = 32
GROUPS = 64
ROWS = 256
N_CHAN = 16
N_TM = 8
WATER = 1.0
EPS = 1e-06
F32 = jnp.float32
BF16 = jnp.bfloat16


def forward_rows():
    freq = np.arange(FREQS)[:, None]
    sample = np.arange(SAMPLES)[None, :]
    phase = (freq * sample % SAMPLES) * (2.0 * math.pi / SAMPLES)
    both = np.stack([np.cos(phase), -np.sin(phase)], 0)
    both = both.reshape(2, GROUPS, 4, SAMPLES).transpose(1, 0, 2, 3)
    return both.reshape(2 * FREQS, SAMPLES).astype(np.float32).astype(BF16)


def lag_rows():
    lag = np.arange(LAGS)[:, None]
    freq = np.arange(FREQS)[None, :]
    phase = (lag * freq % SAMPLES) * (2.0 * math.pi / SAMPLES)
    both = np.stack([np.cos(phase), -np.sin(phase)], 0)
    both = both.reshape(2, N_TM, 1, 8, GROUPS, 1, 4)
    parity = np.eye(2).reshape(1, 1, 2, 1, 1, 2, 1)
    return (both * parity).reshape(2, 2 * LAGS, 2 * FREQS).astype(np.float32).astype(BF16)


def taper_row():
    pos = np.arange(SAMPLES)
    taper = 0.5 - 0.5 * np.cos((pos + 0.5) * (2.0 * math.pi / SAMPLES))
    return taper.astype(np.float32).reshape(1, SAMPLES)


CHUNK = 32
PITCH = 40
PART = 4


def whiten_kernel(
    traces, taper_hbm, table_hbm, out, raw, taper, table, tapered, white_rows, small_sems, in_sems, out_sems
):
    taper_copy = pltpu.make_async_copy(taper_hbm, taper, small_sems.at[0])
    table_copy = pltpu.make_async_copy(table_hbm, table, small_sems.at[1])

    def arrival(chunk):
        rows = pl.ds(chunk * CHUNK, CHUNK)
        return pltpu.make_async_copy(traces.at[rows], raw.at[rows], in_sems.at[chunk])

    def departure(part):
        rows = pl.ds(pl.multiple_of(part * PART * 16, PART * 16), PART * 16)
        return pltpu.make_async_copy(
            white_rows.at[:, rows, :], out.at[:, rows, :], out_sems.at[part]
        )

    taper_copy.start()
    for chunk in range(CH // CHUNK):
        arrival(chunk).start()
    table_copy.start()
    taper_copy.wait()

    def taper_step(chunk, carry):
        arrival(chunk).wait()
        for half in range(CHUNK // 8):
            first = chunk * CHUNK + half * 8
            rows = raw[pl.ds(first, 8)].astype(F32)
            rows = rows - jnp.mean(rows, axis=2, keepdims=True)
            rows = rows * taper[...].reshape(1, 1, SAMPLES)
            for inner in range(8):
                place = pl.ds((first + inner) * PITCH, WIN)
                for tile in range(4):
                    tapered[tile, place, :] = rows[inner, :, tile * 128 : tile * 128 + 128]
        return carry

    lax.fori_loop(0, CH // CHUNK, taper_step, 0)
    table_copy.wait()

    def window_pairs(part, carry):
        for pair in [part * PART + inner for inner in range(PART)]:
            columns = []
            for half in range(2):
                tiles = [
                    tapered[tile, pl.ds(pair * 2 + half, CH, stride=PITCH), :]
                    for tile in range(4)
                ]
                columns.append(jnp.concatenate(tiles, axis=1).astype(BF16))
            columns = jnp.concatenate(columns, axis=0)
            spec = lax.dot_general(
                table[...], columns, (((1,), (1,)), ((), ())), preferred_element_type=F32
            ).reshape(GROUPS, 8, 2 * CH)
            square = spec * spec
            level = jnp.sum(jnp.sum(square, axis=0), axis=0, keepdims=True) * (1.0 / FREQS)
            power = square + pltpu.roll(square, 4, 1)
            white = spec * lax.rsqrt(power + (WATER * level + EPS).reshape(1, 1, 2 * CH))
            white = jnp.concatenate([white[:, :, :CH], white[:, :, CH:]], axis=1)
            white_rows[:, pl.ds(pl.multiple_of(pair * 16, 16), 16), :] = white.astype(BF16)
        departure(part).start()
        return carry

    lax.fori_loop(0, WIN // 2 // PART, window_pairs, 0)
    for part in range(WIN // 2 // PART):
        departure(part).wait()


def whiten(traces):
    return pl.pallas_call(
        whiten_kernel,
        out_shape=jax.ShapeDtypeStruct((GROUPS, ROWS, CH), BF16),
        in_specs=[pl.BlockSpec(memory_space=pl.ANY)] * 3,
        out_specs=pl.BlockSpec(memory_space=pl.ANY),
        scratch_shapes=[
            pltpu.VMEM((CH, WIN, SAMPLES), BF16),
            pltpu.VMEM((1, SAMPLES), F32),
            pltpu.VMEM((2 * FREQS, SAMPLES), BF16),
            pltpu.VMEM((4, CH * PITCH, 128), F32),
            pltpu.VMEM((GROUPS, ROWS, CH), BF16),
            pltpu.SemaphoreType.DMA((2,)),
            pltpu.SemaphoreType.DMA((CH // CHUNK,)),
            pltpu.SemaphoreType.DMA((WIN // 2 // PART,)),
        ],
        compiler_params=pltpu.CompilerParams(vmem_limit_bytes=60 * 2**20),
        cost_estimate=pl.CostEstimate(flops=2 * 2**30, bytes_accessed=2**23, transcendentals=2**20),
        name="whiten",
    )(traces, jnp.asarray(taper_row()), jnp.asarray(forward_rows()))


def expand_kernel(spec, out, wide):
    lane = lax.broadcasted_iota(jnp.int32, (CH, ROWS), 1)
    for part in range(spec.shape[0]):
        turned = spec[part].astype(F32).T
        for f in range(4):
            kept = jnp.where(lane % 4 == f, turned, 0.0)
            for tile in range(2):
                wide[tile, pl.ds(f, CH, stride=4), :] = kept[:, tile * 128 : tile * 128 + 128]
        for tile in range(2):
            out[part, :, tile * 128 : tile * 128 + 128] = wide[tile].astype(BF16)


def expand(spec):
    per = 4
    return pl.pallas_call(
        expand_kernel,
        grid=(GROUPS // per,),
        out_shape=jax.ShapeDtypeStruct((GROUPS, 4 * CH, ROWS), BF16),
        in_specs=[pl.BlockSpec((per, ROWS, CH), lambda g: (g, 0, 0))],
        out_specs=pl.BlockSpec((per, 4 * CH, ROWS), lambda g: (g, 0, 0)),
        scratch_shapes=[pltpu.VMEM((2, 4 * CH, 128), F32)],
        compiler_params=pltpu.CompilerParams(vmem_limit_bytes=32 * 2**20),
        cost_estimate=pl.CostEstimate(flops=2**26, bytes_accessed=20 * 2**20, transcendentals=0),
        name="expand",
    )(spec)


def correlate_kernel(steps, own_hbm, partner_hbm, table, *refs):
    outs = refs[:-5]
    own, partner, cross, own_sems, partner_sems = refs[-5:]
    step = pl.program_id(0)
    per = GROUPS // steps
    sub = lax.broadcasted_iota(jnp.int32, (WIN, 8, CH), 1)

    def arrivals(chunk):
        groups = pl.ds(chunk * per, per)
        return (
            pltpu.make_async_copy(own_hbm.at[groups], own.at[groups], own_sems.at[chunk]),
            pltpu.make_async_copy(
                partner_hbm.at[groups], partner.at[groups], partner_sems.at[chunk]
            ),
        )

    @pl.when(step == 0)
    def _():
        for chunk in range(steps):
            for copy in arrivals(chunk):
                copy.start()

    @pl.when(step < steps)
    def _():
        for copy in arrivals(step):
            copy.wait()
        for pair in range(per // 2):
            halves = []
            for half in range(2):
                group = step * per + 2 * pair + half
                part = partner[group]
                wide = part.astype(F32).reshape(WIN, 8, CH)
                turned = jnp.where(sub < 4, -1.0, 1.0) * pltpu.roll(wide, 4, 1)
                right = jnp.concatenate([part, turned.reshape(ROWS, CH).astype(BF16)], axis=1)
                prod = jnp.dot(own[group], right, preferred_element_type=F32)
                halves.append(prod.reshape(CH // 2, 8, 2 * CH))
            rows = jnp.concatenate(halves, axis=1).astype(BF16)
            first = pl.multiple_of((step * (per // 2) + pair) * 16, 16)
            cross[:, pl.ds(first, 16), :] = rows

    @pl.when(step >= steps)
    def _():
        scale = 1.0 / math.sqrt(FREQS * WIN * N_TM)
        chunk = outs[0].shape[1]
        base = (step - steps) * chunk

        def channel_pairs(idx, carry):
            first, second = cross[base + 2 * idx], cross[base + 2 * idx + 1]
            even = jnp.concatenate([first[:, :CH], second[:, :CH]], axis=1)
            odd = jnp.concatenate([first[:, CH:], second[:, CH:]], axis=1)
            even = jnp.dot(table[0], even, preferred_element_type=F32)
            odd = jnp.dot(table[1], odd, preferred_element_type=F32)
            for sign in range(len(outs) // 4):
                value = (even - odd if sign else even + odd) * scale
                value = value.astype(BF16).reshape(4, 2, 16, 2 * CH)
                for shift in range(4):
                    outs[4 * sign + shift][:, 2 * idx] = value[shift, :, :, :CH]
                    outs[4 * sign + shift][:, 2 * idx + 1] = value[shift, :, :, CH:]
            return carry

        lax.fori_loop(0, chunk // 2, channel_pairs, 0, unroll=8)


def correlate(own, partner, table, signs):
    per, chunk = 8, 16
    steps, late = GROUPS // per, CH // 2 // chunk
    block = pl.BlockSpec((2, chunk, 16, CH), lambda g: (0, jnp.maximum(g - steps, 0), 0, 0))
    return pl.pallas_call(
        functools.partial(correlate_kernel, steps),
        grid=(steps + late,),
        out_shape=[jax.ShapeDtypeStruct((2, CH // 2, 16, CH), BF16)] * (4 * signs),
        in_specs=[
            pl.BlockSpec(memory_space=pl.ANY),
            pl.BlockSpec(memory_space=pl.ANY),
            pl.BlockSpec((2, 2 * LAGS, 2 * FREQS), lambda g: (0, 0, 0)),
        ],
        out_specs=[block] * (4 * signs),
        scratch_shapes=[
            pltpu.VMEM((GROUPS, 4 * CH, ROWS), BF16),
            pltpu.VMEM((GROUPS, ROWS, CH), BF16),
            pltpu.VMEM((CH // 2, 2 * FREQS, 2 * CH), BF16),
            pltpu.SemaphoreType.DMA((steps,)),
            pltpu.SemaphoreType.DMA((steps,)),
        ],
        compiler_params=pltpu.CompilerParams(vmem_limit_bytes=56 * 2**20),
        cost_estimate=pl.CostEstimate(flops=2**34, bytes_accessed=24 * 2**20, transcendentals=0),
        name="correlate_both" if signs == 2 else "correlate_one",
    )(own, partner, table)


def pick_kernel(index, source, out, held, in_sems, out_sems):
    blocks = range(held.shape[0])
    into = [
        pltpu.make_async_copy(source.at[index[c]], held.at[c], in_sems.at[c]) for c in blocks
    ]
    away = [pltpu.make_async_copy(held.at[c], out.at[c], out_sems.at[c]) for c in blocks]
    for copy in into:
        copy.start()
    for arrive, leave in zip(into, away):
        arrive.wait()
        leave.start()
    for copy in away:
        copy.wait()


def pick(source, index):
    return pl.pallas_call(
        pick_kernel,
        grid_spec=pltpu.PrefetchScalarGridSpec(
            num_scalar_prefetch=1,
            grid=(1,),
            in_specs=[pl.BlockSpec(memory_space=pltpu.HBM)],
            out_specs=pl.BlockSpec(memory_space=pltpu.HBM),
            scratch_shapes=[
                pltpu.VMEM(source.shape, source.dtype),
                pltpu.SemaphoreType.DMA((source.shape[0],)),
                pltpu.SemaphoreType.DMA((source.shape[0],)),
            ],
        ),
        out_shape=jax.ShapeDtypeStruct(source.shape, source.dtype),
        compiler_params=pltpu.CompilerParams(vmem_limit_bytes=58 * 2**20),
        cost_estimate=pl.CostEstimate(
            flops=0, bytes_accessed=2 * source.size * source.dtype.itemsize, transcendentals=0
        ),
        name="pick",
    )(index, source)


def at(values, index):
    hit = index[:, None] == jnp.arange(N_CHAN, dtype=jnp.int32)[None, :]
    return jnp.sum(jnp.where(hit, values[None, :], 0), axis=1)


def orient(pairing):
    zero, one = pairing[0], pairing[1]
    hop = at(one, zero)
    least = jnp.arange(N_CHAN, dtype=jnp.int32)
    for _ in range(3):
        least = jnp.minimum(least, at(least, hop))
        hop = at(hop, hop)
    handles_zero = least < at(least, zero)
    return handles_zero, jnp.where(handles_zero, zero, one), jnp.where(handles_zero, one, zero)


def over_chan(blocks):
    return lax.all_to_all(blocks, "chan", split_axis=0, concat_axis=0, tiled=True)


def sent_over_x(parts):
    got = [parts[0]]
    for shift in (2, 1, 3):
        route = [(x * 2 + y, (x + shift) % 4 * 2 + y) for x in range(4) for y in range(2)]
        got.append(lax.ppermute(parts[shift], "tm", route))
    return got


def sum_of(blocks):
    total = blocks[0].astype(F32)
    for block in blocks[1:]:
        total = total + block.astype(F32)
    return total


def sum_over_y(halves):
    mine = lax.axis_index("tm") % 2
    other = lax.dynamic_index_in_dim(halves, 1 - mine, 0, keepdims=False).astype(BF16)
    other = lax.ppermute(other, "tm", [(t, t ^ 1) for t in range(N_TM)])
    return lax.dynamic_index_in_dim(halves, mine, 0, keepdims=False) + other.astype(F32)


def body(traces, pairing):
    spec = whiten(traces)
    spread = over_chan(spec.reshape(N_CHAN, GROUPS // N_CHAN * ROWS, CH))
    own = expand(spec)
    handles_zero, handled, other = orient(pairing)
    table = jnp.asarray(np.concatenate([lag_rows()] * 2, axis=1))
    table = lax.dynamic_slice_in_dim(table, lax.axis_index("tm") // 2 * 32, 2 * LAGS, 1)
    spread, own, handled, other, table = lax.optimization_barrier(
        (spread, own, handled, other, table)
    )
    first = over_chan(pick(spread, handled)).reshape(GROUPS, ROWS, CH)
    second = over_chan(pick(spread, pairing[2])).reshape(GROUPS, ROWS, CH)
    pair_parts = correlate(own, first, table, 2)
    behind = sum_over_y(sum_of(sent_over_x(pair_parts[4:])))
    pair_blocks = sent_over_x(pair_parts[:4])
    last_parts = correlate(own, second, table, 1)
    behind, pair_blocks, last_parts = lax.optimization_barrier((behind, pair_blocks, last_parts))
    behind = over_chan(behind.reshape(N_CHAN, 64, CH).astype(BF16))
    last_blocks = sent_over_x(last_parts)
    behind = behind.at[other].get(mode="promise_in_bounds")
    pair_blocks = lax.optimization_barrier((pair_blocks, behind))[0]
    last_blocks = lax.optimization_barrier((last_blocks, behind))[0]
    behind = over_chan(behind)
    ahead = sum_over_y(sum_of(pair_blocks))
    last = sum_over_y(sum_of(last_blocks))

    def lags_first(value):
        return value.reshape(CH, 8, CH).transpose(1, 0, 2)

    forward = lags_first(ahead)
    backward = behind.astype(F32).reshape(CH, 8, CH).transpose(1, 2, 0)
    mine = lax.dynamic_index_in_dim(handles_zero, lax.axis_index("chan"), 0, keepdims=False)
    return jnp.stack(
        [
            jnp.where(mine, forward, backward),
            jnp.where(mine, backward, forward),
            lags_first(last),
        ]
    )


def solution(mesh):
    return jax.shard_map(
        body,
        mesh=mesh,
        in_specs=(P("chan", "tm", None), P()),
        out_specs=P(None, "tm", "chan", None),
        check_vma=False,
    )
```

```python
import functools
import math

import jax
import jax.numpy as jnp
import numpy as np
from jax import lax
from jax.experimental import pallas as pl
from jax.experimental.pallas import tpu as pltpu
from jax.sharding import PartitionSpec as P

FREQS = 256
SAMPLES = 512
LAGS = 64
CH = 128
WIN = 32
GROUPS = 64
ROWS = 256
N_CHAN = 16
N_TM = 8
WATER = 1.0
EPS = 1e-06
F32 = jnp.float32
BF16 = jnp.bfloat16


def forward_rows():
    freq = np.arange(FREQS)[:, None]
    sample = np.arange(SAMPLES)[None, :]
    phase = (freq * sample % SAMPLES) * (2.0 * math.pi / SAMPLES)
    both = np.stack([np.cos(phase), -np.sin(phase)], 0)
    both = both.reshape(2, GROUPS, 4, SAMPLES).transpose(1, 0, 2, 3)
    return both.reshape(2 * FREQS, SAMPLES).astype(np.float32).astype(BF16)


def lag_rows():
    lag = np.arange(LAGS)[:, None]
    freq = np.arange(FREQS)[None, :]
    phase = (lag * freq % SAMPLES) * (2.0 * math.pi / SAMPLES)
    both = np.stack([np.cos(phase), -np.sin(phase)], 0)
    both = both.reshape(2, N_TM, 1, 8, GROUPS, 1, 4)
    parity = np.eye(2).reshape(1, 1, 2, 1, 1, 2, 1)
    return (both * parity).reshape(2, 2 * LAGS, 2 * FREQS).astype(np.float32).astype(BF16)


def taper_row():
    pos = np.arange(SAMPLES)
    taper = 0.5 - 0.5 * np.cos((pos + 0.5) * (2.0 * math.pi / SAMPLES))
    return taper.astype(np.float32).reshape(1, SAMPLES)


CHUNK = 32
PITCH = 40
PART = 4


def whiten_kernel(
    traces, taper_hbm, table_hbm, out, raw, taper, table, tapered, white_rows, small_sems, in_sems, out_sems
):
    taper_copy = pltpu.make_async_copy(taper_hbm, taper, small_sems.at[0])
    table_copy = pltpu.make_async_copy(table_hbm, table, small_sems.at[1])

    def arrival(chunk):
        rows = pl.ds(chunk * CHUNK, CHUNK)
        return pltpu.make_async_copy(traces.at[rows], raw.at[rows], in_sems.at[chunk])

    def departure(part):
        rows = pl.ds(pl.multiple_of(part * PART * 16, PART * 16), PART * 16)
        return pltpu.make_async_copy(
            white_rows.at[:, rows, :], out.at[:, rows, :], out_sems.at[part]
        )

    taper_copy.start()
    for chunk in range(CH // CHUNK):
        arrival(chunk).start()
    table_copy.start()
    taper_copy.wait()

    def taper_step(chunk, carry):
        arrival(chunk).wait()
        for half in range(CHUNK // 8):
            first = chunk * CHUNK + half * 8
            rows = raw[pl.ds(first, 8)].astype(F32)
            rows = rows - jnp.mean(rows, axis=2, keepdims=True)
            rows = rows * taper[...].reshape(1, 1, SAMPLES)
            for inner in range(8):
                place = pl.ds((first + inner) * PITCH, WIN)
                for tile in range(4):
                    tapered[tile, place, :] = rows[inner, :, tile * 128 : tile * 128 + 128]
        return carry

    lax.fori_loop(0, CH // CHUNK, taper_step, 0)
    table_copy.wait()

    def window_pairs(part, carry):
        for pair in [part * PART + inner for inner in range(PART)]:
            columns = []
            for half in range(2):
                tiles = [
                    tapered[tile, pl.ds(pair * 2 + half, CH, stride=PITCH), :]
                    for tile in range(4)
                ]
                columns.append(jnp.concatenate(tiles, axis=1).astype(BF16))
            columns = jnp.concatenate(columns, axis=0)
            spec = lax.dot_general(
                table[...], columns, (((1,), (1,)), ((), ())), preferred_element_type=F32
            ).reshape(GROUPS, 8, 2 * CH)
            square = spec * spec
            level = jnp.sum(jnp.sum(square, axis=0), axis=0, keepdims=True) * (1.0 / FREQS)
            power = square + pltpu.roll(square, 4, 1)
            white = spec * lax.rsqrt(power + (WATER * level + EPS).reshape(1, 1, 2 * CH))
            white = jnp.concatenate([white[:, :, :CH], white[:, :, CH:]], axis=1)
            white_rows[:, pl.ds(pl.multiple_of(pair * 16, 16), 16), :] = white.astype(BF16)
        departure(part).start()
        return carry

    lax.fori_loop(0, WIN // 2 // PART, window_pairs, 0)
    for part in range(WIN // 2 // PART):
        departure(part).wait()


def whiten(traces):
    return pl.pallas_call(
        whiten_kernel,
        out_shape=jax.ShapeDtypeStruct((GROUPS, ROWS, CH), BF16),
        in_specs=[pl.BlockSpec(memory_space=pl.ANY)] * 3,
        out_specs=pl.BlockSpec(memory_space=pl.ANY),
        scratch_shapes=[
            pltpu.VMEM((CH, WIN, SAMPLES), BF16),
            pltpu.VMEM((1, SAMPLES), F32),
            pltpu.VMEM((2 * FREQS, SAMPLES), BF16),
            pltpu.VMEM((4, CH * PITCH, 128), F32),
            pltpu.VMEM((GROUPS, ROWS, CH), BF16),
            pltpu.SemaphoreType.DMA((2,)),
            pltpu.SemaphoreType.DMA((CH // CHUNK,)),
            pltpu.SemaphoreType.DMA((WIN // 2 // PART,)),
        ],
        compiler_params=pltpu.CompilerParams(vmem_limit_bytes=60 * 2**20),
        cost_estimate=pl.CostEstimate(flops=2 * 2**30, bytes_accessed=2**23, transcendentals=2**20),
        name="whiten",
    )(traces, jnp.asarray(taper_row()), jnp.asarray(forward_rows()))


def expand_kernel(spec, out, wide):
    lane = lax.broadcasted_iota(jnp.int32, (CH, ROWS), 1)
    for part in range(spec.shape[0]):
        turned = spec[part].astype(F32).T
        for f in range(4):
            kept = jnp.where(lane % 4 == f, turned, 0.0)
            for tile in range(2):
                wide[tile, pl.ds(f, CH, stride=4), :] = kept[:, tile * 128 : tile * 128 + 128]
        for tile in range(2):
            out[part, :, tile * 128 : tile * 128 + 128] = wide[tile].astype(BF16)


def expand(spec):
    per = 4
    return pl.pallas_call(
        expand_kernel,
        grid=(GROUPS // per,),
        out_shape=jax.ShapeDtypeStruct((GROUPS, 4 * CH, ROWS), BF16),
        in_specs=[pl.BlockSpec((per, ROWS, CH), lambda g: (g, 0, 0))],
        out_specs=pl.BlockSpec((per, 4 * CH, ROWS), lambda g: (g, 0, 0)),
        scratch_shapes=[pltpu.VMEM((2, 4 * CH, 128), F32)],
        compiler_params=pltpu.CompilerParams(vmem_limit_bytes=32 * 2**20),
        cost_estimate=pl.CostEstimate(flops=2**26, bytes_accessed=20 * 2**20, transcendentals=0),
        name="expand",
    )(spec)


def correlate_kernel(steps, own_hbm, partner_hbm, table, *refs):
    outs = refs[:4]
    own, partner, cross, own_sems, partner_sems = refs[4:]
    step = pl.program_id(0)
    per = GROUPS // steps
    sub = lax.broadcasted_iota(jnp.int32, (WIN, 8, CH), 1)

    def arrivals(chunk):
        groups = pl.ds(chunk * per, per)
        return (
            pltpu.make_async_copy(own_hbm.at[groups], own.at[groups], own_sems.at[chunk]),
            pltpu.make_async_copy(
                partner_hbm.at[groups], partner.at[groups], partner_sems.at[chunk]
            ),
        )

    @pl.when(step == 0)
    def _():
        for chunk in range(steps):
            for copy in arrivals(chunk):
                copy.start()

    @pl.when(step < steps)
    def _():
        for copy in arrivals(step):
            copy.wait()
        for pair in range(per // 2):
            halves = []
            for half in range(2):
                group = step * per + 2 * pair + half
                part = partner[group]
                wide = part.astype(F32).reshape(WIN, 8, CH)
                turned = jnp.where(sub < 4, -1.0, 1.0) * pltpu.roll(wide, 4, 1)
                right = jnp.concatenate([part, turned.reshape(ROWS, CH).astype(BF16)], axis=1)
                prod = jnp.dot(own[group], right, preferred_element_type=F32)
                halves.append(prod.reshape(CH // 2, 8, 2 * CH))
            rows = jnp.concatenate(halves, axis=1).astype(BF16)
            first = pl.multiple_of((step * (per // 2) + pair) * 16, 16)
            cross[:, pl.ds(first, 16), :] = rows

    @pl.when(step >= steps)
    def _():
        scale = 1.0 / math.sqrt(FREQS * WIN * N_TM)
        signs, chunk = outs[0].shape[1:3]
        base = (step - steps) * chunk

        def channel_pairs(idx, carry):
            first, second = cross[base + 2 * idx], cross[base + 2 * idx + 1]
            even = jnp.concatenate([first[:, :CH], second[:, :CH]], axis=1)
            odd = jnp.concatenate([first[:, CH:], second[:, CH:]], axis=1)
            even = jnp.dot(table[0], even, preferred_element_type=F32)
            odd = jnp.dot(table[1], odd, preferred_element_type=F32)
            for sign in range(signs):
                value = (even - odd if sign else even + odd) * scale
                value = value.astype(BF16).reshape(4, 2, 16, 2 * CH)
                for shift in range(4):
                    outs[shift][:, sign, 2 * idx] = value[shift, :, :, :CH]
                    outs[shift][:, sign, 2 * idx + 1] = value[shift, :, :, CH:]
            return carry

        lax.fori_loop(0, chunk // 2, channel_pairs, 0, unroll=8)


def correlate(own, partner, table, signs):
    per, chunk = 8, 16
    steps, late = GROUPS // per, CH // 2 // chunk
    block = pl.BlockSpec(
        (2, signs, chunk, 16, CH), lambda g: (0, 0, jnp.maximum(g - steps, 0), 0, 0)
    )
    return pl.pallas_call(
        functools.partial(correlate_kernel, steps),
        grid=(steps + late,),
        out_shape=[jax.ShapeDtypeStruct((2, signs, CH // 2, 16, CH), BF16)] * 4,
        in_specs=[
            pl.BlockSpec(memory_space=pl.ANY),
            pl.BlockSpec(memory_space=pl.ANY),
            pl.BlockSpec((2, 2 * LAGS, 2 * FREQS), lambda g: (0, 0, 0)),
        ],
        out_specs=[block] * 4,
        scratch_shapes=[
            pltpu.VMEM((GROUPS, 4 * CH, ROWS), BF16),
            pltpu.VMEM((GROUPS, ROWS, CH), BF16),
            pltpu.VMEM((CH // 2, 2 * FREQS, 2 * CH), BF16),
            pltpu.SemaphoreType.DMA((steps,)),
            pltpu.SemaphoreType.DMA((steps,)),
        ],
        compiler_params=pltpu.CompilerParams(vmem_limit_bytes=56 * 2**20),
        cost_estimate=pl.CostEstimate(flops=2**34, bytes_accessed=24 * 2**20, transcendentals=0),
        name="correlate_both" if signs == 2 else "correlate_one",
    )(own, partner, table)


def pick_kernel(index, source, out, held, in_sems, out_sems):
    blocks = range(held.shape[0])
    into = [
        pltpu.make_async_copy(source.at[index[c]], held.at[c], in_sems.at[c]) for c in blocks
    ]
    away = [pltpu.make_async_copy(held.at[c], out.at[c], out_sems.at[c]) for c in blocks]
    for copy in into:
        copy.start()
    for arrive, leave in zip(into, away):
        arrive.wait()
        leave.start()
    for copy in away:
        copy.wait()


def pick(source, index):
    return pl.pallas_call(
        pick_kernel,
        grid_spec=pltpu.PrefetchScalarGridSpec(
            num_scalar_prefetch=1,
            grid=(1,),
            in_specs=[pl.BlockSpec(memory_space=pltpu.HBM)],
            out_specs=pl.BlockSpec(memory_space=pltpu.HBM),
            scratch_shapes=[
                pltpu.VMEM(source.shape, source.dtype),
                pltpu.SemaphoreType.DMA((source.shape[0],)),
                pltpu.SemaphoreType.DMA((source.shape[0],)),
            ],
        ),
        out_shape=jax.ShapeDtypeStruct(source.shape, source.dtype),
        compiler_params=pltpu.CompilerParams(vmem_limit_bytes=58 * 2**20),
        cost_estimate=pl.CostEstimate(
            flops=0, bytes_accessed=2 * source.size * source.dtype.itemsize, transcendentals=0
        ),
        name="pick",
    )(index, source)


def at(values, index):
    hit = index[:, None] == jnp.arange(N_CHAN, dtype=jnp.int32)[None, :]
    return jnp.sum(jnp.where(hit, values[None, :], 0), axis=1)


def orient(pairing):
    zero, one = pairing[0], pairing[1]
    hop = at(one, zero)
    least = jnp.arange(N_CHAN, dtype=jnp.int32)
    for _ in range(3):
        least = jnp.minimum(least, at(least, hop))
        hop = at(hop, hop)
    handles_zero = least < at(least, zero)
    return handles_zero, jnp.where(handles_zero, zero, one), jnp.where(handles_zero, one, zero)


def over_chan(blocks):
    return lax.all_to_all(blocks, "chan", split_axis=0, concat_axis=0, tiled=True)


def sent_over_x(parts):
    got = [parts[0]]
    for shift in (2, 1, 3):
        route = [(x * 2 + y, (x + shift) % 4 * 2 + y) for x in range(4) for y in range(2)]
        got.append(lax.ppermute(parts[shift], "tm", route))
    return got


def sum_of(blocks):
    total = blocks[0].astype(F32)
    for block in blocks[1:]:
        total = total + block.astype(F32)
    return total


def sum_over_y(halves):
    mine = lax.axis_index("tm") % 2
    other = lax.dynamic_index_in_dim(halves, 1 - mine, 0, keepdims=False).astype(BF16)
    other = lax.ppermute(other, "tm", [(t, t ^ 1) for t in range(N_TM)])
    return lax.dynamic_index_in_dim(halves, mine, 0, keepdims=False) + other.astype(F32)


def body(traces, pairing):
    spec = whiten(traces)
    spread = over_chan(spec.reshape(N_CHAN, GROUPS // N_CHAN * ROWS, CH))
    own = expand(spec)
    handles_zero, handled, other = orient(pairing)
    table = jnp.asarray(np.concatenate([lag_rows()] * 2, axis=1))
    table = lax.dynamic_slice_in_dim(table, lax.axis_index("tm") // 2 * 32, 2 * LAGS, 1)
    spread, own, handled, other, table = lax.optimization_barrier(
        (spread, own, handled, other, table)
    )
    first = over_chan(pick(spread, handled)).reshape(GROUPS, ROWS, CH)
    second = over_chan(pick(spread, pairing[2])).reshape(GROUPS, ROWS, CH)
    pair_blocks = sent_over_x(correlate(own, first, table, 2))
    last_parts = correlate(own, second, table, 1)
    pair_blocks, last_parts = lax.optimization_barrier((pair_blocks, last_parts))
    pair_halves = sum_of(pair_blocks)
    last_blocks = sent_over_x(last_parts)
    behind = sum_over_y(pair_halves[:, 1])
    behind = over_chan(behind.reshape(N_CHAN, 64, CH).astype(BF16))
    behind = behind.at[other].get(mode="promise_in_bounds")
    last_blocks = lax.optimization_barrier((last_blocks, behind))[0]
    pair_halves = lax.optimization_barrier((pair_halves, behind))[0]
    behind = over_chan(behind)
    ahead = sum_over_y(pair_halves[:, 0])
    last = sum_over_y(sum_of(last_blocks)[:, 0])

    def lags_first(value):
        return value.reshape(CH, 8, CH).transpose(1, 0, 2)

    forward = lags_first(ahead)
    backward = behind.astype(F32).reshape(CH, 8, CH).transpose(1, 2, 0)
    mine = lax.dynamic_index_in_dim(handles_zero, lax.axis_index("chan"), 0, keepdims=False)
    return jnp.stack(
        [
            jnp.where(mine, forward, backward),
            jnp.where(mine, backward, forward),
            lags_first(last),
        ]
    )


def solution(mesh):
    return jax.shard_map(
        body,
        mesh=mesh,
        in_specs=(P("chan", "tm", None), P()),
        out_specs=P(None, "tm", "chan", None),
        check_vma=False,
    )
```

```python
import functools
import math

import jax
import jax.numpy as jnp
import numpy as np
from jax import lax
from jax.experimental import pallas as pl
from jax.experimental.pallas import tpu as pltpu
from jax.sharding import PartitionSpec as P

FREQS = 256
SAMPLES = 512
LAGS = 64
CH = 128
WIN = 32
GROUPS = 64
ROWS = 256
N_CHAN = 16
N_TM = 8
WATER = 1.0
EPS = 1e-06
F32 = jnp.float32
BF16 = jnp.bfloat16


def forward_rows():
    freq = np.arange(FREQS)[:, None]
    sample = np.arange(SAMPLES)[None, :]
    phase = (freq * sample % SAMPLES) * (2.0 * math.pi / SAMPLES)
    both = np.stack([np.cos(phase), -np.sin(phase)], 0)
    both = both.reshape(2, GROUPS, 4, SAMPLES).transpose(1, 0, 2, 3)
    return both.reshape(2 * FREQS, SAMPLES).astype(np.float32).astype(BF16)


def lag_rows():
    lag = np.arange(LAGS)[:, None]
    freq = np.arange(FREQS)[None, :]
    phase = (lag * freq % SAMPLES) * (2.0 * math.pi / SAMPLES)
    both = np.stack([np.cos(phase), -np.sin(phase)], 0)
    both = both.reshape(2, N_TM, 1, 8, GROUPS, 1, 4)
    parity = np.eye(2).reshape(1, 1, 2, 1, 1, 2, 1)
    return (both * parity).reshape(2, 2 * LAGS, 2 * FREQS).astype(np.float32).astype(BF16)


def taper_row():
    pos = np.arange(SAMPLES)
    taper = 0.5 - 0.5 * np.cos((pos + 0.5) * (2.0 * math.pi / SAMPLES))
    return taper.astype(np.float32).reshape(1, SAMPLES)


CHUNK = 32
PITCH = 40
PART = 4


def whiten_kernel(
    traces, taper_hbm, table_hbm, out, raw, taper, table, tapered, white_rows, small_sems, in_sems, out_sems
):
    taper_copy = pltpu.make_async_copy(taper_hbm, taper, small_sems.at[0])
    table_copy = pltpu.make_async_copy(table_hbm, table, small_sems.at[1])

    def arrival(chunk):
        rows = pl.ds(chunk * CHUNK, CHUNK)
        return pltpu.make_async_copy(traces.at[rows], raw.at[rows], in_sems.at[chunk])

    def departure(part):
        rows = pl.ds(pl.multiple_of(part * PART * 16, PART * 16), PART * 16)
        return pltpu.make_async_copy(
            white_rows.at[:, rows, :], out.at[:, rows, :], out_sems.at[part]
        )

    taper_copy.start()
    for chunk in range(CH // CHUNK):
        arrival(chunk).start()
    table_copy.start()
    taper_copy.wait()

    def taper_step(chunk, carry):
        arrival(chunk).wait()
        for half in range(CHUNK // 8):
            first = chunk * CHUNK + half * 8
            rows = raw[pl.ds(first, 8)].astype(F32)
            rows = rows - jnp.mean(rows, axis=2, keepdims=True)
            rows = rows * taper[...].reshape(1, 1, SAMPLES)
            for inner in range(8):
                place = pl.ds((first + inner) * PITCH, WIN)
                for tile in range(4):
                    tapered[tile, place, :] = rows[inner, :, tile * 128 : tile * 128 + 128]
        return carry

    lax.fori_loop(0, CH // CHUNK, taper_step, 0)
    table_copy.wait()

    def window_pairs(part, carry):
        for pair in [part * PART + inner for inner in range(PART)]:
            columns = []
            for half in range(2):
                tiles = [
                    tapered[tile, pl.ds(pair * 2 + half, CH, stride=PITCH), :]
                    for tile in range(4)
                ]
                columns.append(jnp.concatenate(tiles, axis=1).astype(BF16))
            columns = jnp.concatenate(columns, axis=0)
            spec = lax.dot_general(
                table[...], columns, (((1,), (1,)), ((), ())), preferred_element_type=F32
            ).reshape(GROUPS, 8, 2 * CH)
            square = spec * spec
            level = jnp.sum(jnp.sum(square, axis=0), axis=0, keepdims=True) * (1.0 / FREQS)
            power = square + pltpu.roll(square, 4, 1)
            white = spec * lax.rsqrt(power + (WATER * level + EPS).reshape(1, 1, 2 * CH))
            white = jnp.concatenate([white[:, :, :CH], white[:, :, CH:]], axis=1)
            white_rows[:, pl.ds(pl.multiple_of(pair * 16, 16), 16), :] = white.astype(BF16)
        departure(part).start()
        return carry

    lax.fori_loop(0, WIN // 2 // PART, window_pairs, 0)
    for part in range(WIN // 2 // PART):
        departure(part).wait()


def whiten(traces):
    return pl.pallas_call(
        whiten_kernel,
        out_shape=jax.ShapeDtypeStruct((GROUPS, ROWS, CH), BF16),
        in_specs=[pl.BlockSpec(memory_space=pl.ANY)] * 3,
        out_specs=pl.BlockSpec(memory_space=pl.ANY),
        scratch_shapes=[
            pltpu.VMEM((CH, WIN, SAMPLES), BF16),
            pltpu.VMEM((1, SAMPLES), F32),
            pltpu.VMEM((2 * FREQS, SAMPLES), BF16),
            pltpu.VMEM((4, CH * PITCH, 128), F32),
            pltpu.VMEM((GROUPS, ROWS, CH), BF16),
            pltpu.SemaphoreType.DMA((2,)),
            pltpu.SemaphoreType.DMA((CH // CHUNK,)),
            pltpu.SemaphoreType.DMA((WIN // 2 // PART,)),
        ],
        compiler_params=pltpu.CompilerParams(vmem_limit_bytes=60 * 2**20),
        cost_estimate=pl.CostEstimate(flops=2 * 2**30, bytes_accessed=2**23, transcendentals=2**20),
        name="whiten",
    )(traces, jnp.asarray(taper_row()), jnp.asarray(forward_rows()))


def expand_kernel(spec, out, wide):
    lane = lax.broadcasted_iota(jnp.int32, (CH, ROWS), 1)
    for part in range(spec.shape[0]):
        turned = spec[part].astype(F32).T
        for f in range(4):
            kept = jnp.where(lane % 4 == f, turned, 0.0)
            for tile in range(2):
                wide[tile, pl.ds(f, CH, stride=4), :] = kept[:, tile * 128 : tile * 128 + 128]
        for tile in range(2):
            out[part, :, tile * 128 : tile * 128 + 128] = wide[tile].astype(BF16)


def expand(spec):
    per = 4
    return pl.pallas_call(
        expand_kernel,
        grid=(GROUPS // per,),
        out_shape=jax.ShapeDtypeStruct((GROUPS, 4 * CH, ROWS), BF16),
        in_specs=[pl.BlockSpec((per, ROWS, CH), lambda g: (g, 0, 0))],
        out_specs=pl.BlockSpec((per, 4 * CH, ROWS), lambda g: (g, 0, 0)),
        scratch_shapes=[pltpu.VMEM((2, 4 * CH, 128), F32)],
        compiler_params=pltpu.CompilerParams(vmem_limit_bytes=32 * 2**20),
        cost_estimate=pl.CostEstimate(flops=2**26, bytes_accessed=20 * 2**20, transcendentals=0),
        name="expand",
    )(spec)


def correlate_kernel(steps, own_hbm, partner_hbm, table, *refs):
    outs = refs[:4]
    own, partner, cross, own_sems, partner_sems = refs[4:]
    step = pl.program_id(0)
    per = GROUPS // steps
    sub = lax.broadcasted_iota(jnp.int32, (WIN, 8, CH), 1)

    def arrivals(chunk):
        groups = pl.ds(chunk * per, per)
        return (
            pltpu.make_async_copy(own_hbm.at[groups], own.at[groups], own_sems.at[chunk]),
            pltpu.make_async_copy(
                partner_hbm.at[groups], partner.at[groups], partner_sems.at[chunk]
            ),
        )

    @pl.when(step == 0)
    def _():
        for chunk in range(steps):
            for copy in arrivals(chunk):
                copy.start()

    @pl.when(step < steps)
    def _():
        for copy in arrivals(step):
            copy.wait()
        for pair in range(per // 2):
            halves = []
            for half in range(2):
                group = step * per + 2 * pair + half
                part = partner[group]
                wide = part.astype(F32).reshape(WIN, 8, CH)
                turned = jnp.where(sub < 4, -1.0, 1.0) * pltpu.roll(wide, 4, 1)
                right = jnp.concatenate([part, turned.reshape(ROWS, CH).astype(BF16)], axis=1)
                prod = jnp.dot(own[group], right, preferred_element_type=F32)
                halves.append(prod.reshape(CH // 2, 8, 2 * CH))
            rows = jnp.concatenate(halves, axis=1).astype(BF16)
            first = pl.multiple_of((step * (per // 2) + pair) * 16, 16)
            cross[:, pl.ds(first, 16), :] = rows

    @pl.when(step >= steps)
    def _():
        scale = 1.0 / math.sqrt(FREQS * WIN * N_TM)
        signs, chunk = outs[0].shape[1:3]
        base = (step - steps) * chunk

        def channel_pairs(idx, carry):
            first, second = cross[base + 2 * idx], cross[base + 2 * idx + 1]
            even = jnp.concatenate([first[:, :CH], second[:, :CH]], axis=1)
            odd = jnp.concatenate([first[:, CH:], second[:, CH:]], axis=1)
            even = jnp.dot(table[0], even, preferred_element_type=F32)
            odd = jnp.dot(table[1], odd, preferred_element_type=F32)
            for sign in range(signs):
                value = (even - odd if sign else even + odd) * scale
                value = value.astype(BF16).reshape(4, 2, 16, 2 * CH)
                for shift in range(4):
                    outs[shift][:, sign, 2 * idx] = value[shift, :, :, :CH]
                    outs[shift][:, sign, 2 * idx + 1] = value[shift, :, :, CH:]
            return carry

        lax.fori_loop(0, chunk // 2, channel_pairs, 0, unroll=8)


def correlate(own, partner, table, signs):
    per, chunk = 8, 16
    steps, late = GROUPS // per, CH // 2 // chunk
    block = pl.BlockSpec(
        (2, signs, chunk, 16, CH), lambda g: (0, 0, jnp.maximum(g - steps, 0), 0, 0)
    )
    return pl.pallas_call(
        functools.partial(correlate_kernel, steps),
        grid=(steps + late,),
        out_shape=[jax.ShapeDtypeStruct((2, signs, CH // 2, 16, CH), BF16)] * 4,
        in_specs=[
            pl.BlockSpec(memory_space=pl.ANY),
            pl.BlockSpec(memory_space=pl.ANY),
            pl.BlockSpec((2, 2 * LAGS, 2 * FREQS), lambda g: (0, 0, 0)),
        ],
        out_specs=[block] * 4,
        scratch_shapes=[
            pltpu.VMEM((GROUPS, 4 * CH, ROWS), BF16),
            pltpu.VMEM((GROUPS, ROWS, CH), BF16),
            pltpu.VMEM((CH // 2, 2 * FREQS, 2 * CH), BF16),
            pltpu.SemaphoreType.DMA((steps,)),
            pltpu.SemaphoreType.DMA((steps,)),
        ],
        compiler_params=pltpu.CompilerParams(vmem_limit_bytes=56 * 2**20),
        cost_estimate=pl.CostEstimate(flops=2**34, bytes_accessed=24 * 2**20, transcendentals=0),
        name="correlate_both" if signs == 2 else "correlate_one",
    )(own, partner, table)


def pick_kernel(index, source, out, held, in_sems, out_sems):
    blocks = range(held.shape[0])
    into = [
        pltpu.make_async_copy(source.at[index[c]], held.at[c], in_sems.at[c]) for c in blocks
    ]
    away = [pltpu.make_async_copy(held.at[c], out.at[c], out_sems.at[c]) for c in blocks]
    for copy in into:
        copy.start()
    for arrive, leave in zip(into, away):
        arrive.wait()
        leave.start()
    for copy in away:
        copy.wait()


def pick(source, index):
    return pl.pallas_call(
        pick_kernel,
        grid_spec=pltpu.PrefetchScalarGridSpec(
            num_scalar_prefetch=1,
            grid=(1,),
            in_specs=[pl.BlockSpec(memory_space=pltpu.HBM)],
            out_specs=pl.BlockSpec(memory_space=pltpu.HBM),
            scratch_shapes=[
                pltpu.VMEM(source.shape, source.dtype),
                pltpu.SemaphoreType.DMA((source.shape[0],)),
                pltpu.SemaphoreType.DMA((source.shape[0],)),
            ],
        ),
        out_shape=jax.ShapeDtypeStruct(source.shape, source.dtype),
        compiler_params=pltpu.CompilerParams(vmem_limit_bytes=58 * 2**20),
        cost_estimate=pl.CostEstimate(
            flops=0, bytes_accessed=2 * source.size * source.dtype.itemsize, transcendentals=0
        ),
        name="pick",
    )(index, source)


def at(values, index):
    hit = index[:, None] == jnp.arange(N_CHAN, dtype=jnp.int32)[None, :]
    return jnp.sum(jnp.where(hit, values[None, :], 0), axis=1)


def orient(pairing):
    zero, one = pairing[0], pairing[1]
    hop = at(one, zero)
    least = jnp.arange(N_CHAN, dtype=jnp.int32)
    for _ in range(3):
        least = jnp.minimum(least, at(least, hop))
        hop = at(hop, hop)
    handles_zero = least < at(least, zero)
    return handles_zero, jnp.where(handles_zero, zero, one), jnp.where(handles_zero, one, zero)


def over_chan(blocks):
    return lax.all_to_all(blocks, "chan", split_axis=0, concat_axis=0, tiled=True)


def sent_over_x(parts):
    got = [parts[0]]
    for shift in (2, 1, 3):
        route = [(x * 2 + y, (x + shift) % 4 * 2 + y) for x in range(4) for y in range(2)]
        got.append(lax.ppermute(parts[shift], "tm", route))
    return got


def sum_of(blocks):
    total = blocks[0].astype(F32)
    for block in blocks[1:]:
        total = total + block.astype(F32)
    return total


def sum_over_y(halves):
    mine = lax.axis_index("tm") % 2
    other = lax.dynamic_index_in_dim(halves, 1 - mine, 0, keepdims=False).astype(BF16)
    other = lax.ppermute(other, "tm", [(t, t ^ 1) for t in range(N_TM)])
    return lax.dynamic_index_in_dim(halves, mine, 0, keepdims=False) + other.astype(F32)


def body(traces, pairing):
    spec = whiten(traces)
    spread = over_chan(spec.reshape(N_CHAN, GROUPS // N_CHAN * ROWS, CH))
    own = expand(spec)
    handles_zero, handled, other = orient(pairing)
    table = jnp.asarray(np.concatenate([lag_rows()] * 2, axis=1))
    table = lax.dynamic_slice_in_dim(table, lax.axis_index("tm") // 2 * 32, 2 * LAGS, 1)
    spread, own, handled, other, table = lax.optimization_barrier(
        (spread, own, handled, other, table)
    )
    first = over_chan(pick(spread, handled)).reshape(GROUPS, ROWS, CH)
    second = over_chan(pick(spread, pairing[2])).reshape(GROUPS, ROWS, CH)
    pair_blocks = sent_over_x(correlate(own, first, table, 2))
    last_parts = correlate(own, second, table, 1)
    pair_blocks, last_parts = lax.optimization_barrier((pair_blocks, last_parts))
    pair_halves = sum_of(pair_blocks)
    last_blocks = sent_over_x(last_parts)
    behind = sum_over_y(pair_halves[:, 1])
    behind = over_chan(behind.reshape(N_CHAN, 64, CH).astype(BF16))
    behind = behind.at[other].get(mode="promise_in_bounds")
    behind = over_chan(behind)
    ahead = sum_over_y(pair_halves[:, 0])
    last = sum_over_y(sum_of(last_blocks)[:, 0])

    def lags_first(value):
        return value.reshape(CH, 8, CH).transpose(1, 0, 2)

    forward = lags_first(ahead)
    backward = behind.astype(F32).reshape(CH, 8, CH).transpose(1, 2, 0)
    mine = lax.dynamic_index_in_dim(handles_zero, lax.axis_index("chan"), 0, keepdims=False)
    return jnp.stack(
        [
            jnp.where(mine, forward, backward),
            jnp.where(mine, backward, forward),
            lags_first(last),
        ]
    )


def solution(mesh):
    return jax.shard_map(
        body,
        mesh=mesh,
        in_specs=(P("chan", "tm", None), P()),
        out_specs=P(None, "tm", "chan", None),
        check_vma=False,
    )
```

```python
import functools
import math

import jax
import jax.numpy as jnp
import numpy as np
from jax import lax
from jax.experimental import pallas as pl
from jax.experimental.pallas import tpu as pltpu
from jax.sharding import PartitionSpec as P

FREQS = 256
SAMPLES = 512
LAGS = 64
CH = 128
WIN = 32
GROUPS = 64
ROWS = 256
N_CHAN = 16
N_TM = 8
WATER = 1.0
EPS = 1e-06
F32 = jnp.float32
BF16 = jnp.bfloat16


def forward_rows():
    freq = np.arange(FREQS)[:, None]
    sample = np.arange(SAMPLES)[None, :]
    phase = (freq * sample % SAMPLES) * (2.0 * math.pi / SAMPLES)
    both = np.stack([np.cos(phase), -np.sin(phase)], 0)
    both = both.reshape(2, GROUPS, 4, SAMPLES).transpose(1, 0, 2, 3)
    return both.reshape(2 * FREQS, SAMPLES).astype(np.float32).astype(BF16)


def lag_rows():
    lag = np.arange(LAGS)[:, None]
    freq = np.arange(FREQS)[None, :]
    phase = (lag * freq % SAMPLES) * (2.0 * math.pi / SAMPLES)
    both = np.stack([np.cos(phase), -np.sin(phase)], 0)
    both = both.reshape(2, N_TM, 1, 8, GROUPS, 1, 4)
    parity = np.eye(2).reshape(1, 1, 2, 1, 1, 2, 1)
    return (both * parity).reshape(2, 2 * LAGS, 2 * FREQS).astype(np.float32).astype(BF16)


def taper_row():
    pos = np.arange(SAMPLES)
    taper = 0.5 - 0.5 * np.cos((pos + 0.5) * (2.0 * math.pi / SAMPLES))
    return taper.astype(np.float32).reshape(1, SAMPLES)


CHUNK = 32
PITCH = 40
PART = 4


def whiten_kernel(
    traces, taper_hbm, table_hbm, out, raw, taper, table, tapered, white_rows, small_sems, in_sems, out_sems
):
    taper_copy = pltpu.make_async_copy(taper_hbm, taper, small_sems.at[0])
    table_copy = pltpu.make_async_copy(table_hbm, table, small_sems.at[1])

    def arrival(chunk):
        rows = pl.ds(chunk * CHUNK, CHUNK)
        return pltpu.make_async_copy(traces.at[rows], raw.at[rows], in_sems.at[chunk])

    def departure(part):
        rows = pl.ds(pl.multiple_of(part * PART * 16, PART * 16), PART * 16)
        return pltpu.make_async_copy(
            white_rows.at[:, rows, :], out.at[:, rows, :], out_sems.at[part]
        )

    taper_copy.start()
    for chunk in range(CH // CHUNK):
        arrival(chunk).start()
    table_copy.start()
    taper_copy.wait()

    def taper_step(chunk, carry):
        arrival(chunk).wait()
        for half in range(CHUNK // 8):
            first = chunk * CHUNK + half * 8
            rows = raw[pl.ds(first, 8)].astype(F32)
            rows = rows - jnp.mean(rows, axis=2, keepdims=True)
            rows = rows * taper[...].reshape(1, 1, SAMPLES)
            for inner in range(8):
                place = pl.ds((first + inner) * PITCH, WIN)
                for tile in range(4):
                    tapered[tile, place, :] = rows[inner, :, tile * 128 : tile * 128 + 128]
        return carry

    lax.fori_loop(0, CH // CHUNK, taper_step, 0)
    table_copy.wait()

    def window_pairs(part, carry):
        for pair in [part * PART + inner for inner in range(PART)]:
            columns = []
            for half in range(2):
                tiles = [
                    tapered[tile, pl.ds(pair * 2 + half, CH, stride=PITCH), :]
                    for tile in range(4)
                ]
                columns.append(jnp.concatenate(tiles, axis=1).astype(BF16))
            columns = jnp.concatenate(columns, axis=0)
            spec = lax.dot_general(
                table[...], columns, (((1,), (1,)), ((), ())), preferred_element_type=F32
            ).reshape(GROUPS, 8, 2 * CH)
            square = spec * spec
            level = jnp.sum(jnp.sum(square, axis=0), axis=0, keepdims=True) * (1.0 / FREQS)
            power = square + pltpu.roll(square, 4, 1)
            white = spec * lax.rsqrt(power + (WATER * level + EPS).reshape(1, 1, 2 * CH))
            white = jnp.concatenate([white[:, :, :CH], white[:, :, CH:]], axis=1)
            white_rows[:, pl.ds(pl.multiple_of(pair * 16, 16), 16), :] = white.astype(BF16)
        departure(part).start()
        return carry

    lax.fori_loop(0, WIN // 2 // PART, window_pairs, 0)
    for part in range(WIN // 2 // PART):
        departure(part).wait()


def whiten(traces):
    return pl.pallas_call(
        whiten_kernel,
        out_shape=jax.ShapeDtypeStruct((GROUPS, ROWS, CH), BF16),
        in_specs=[pl.BlockSpec(memory_space=pl.ANY)] * 3,
        out_specs=pl.BlockSpec(memory_space=pl.ANY),
        scratch_shapes=[
            pltpu.VMEM((CH, WIN, SAMPLES), BF16),
            pltpu.VMEM((1, SAMPLES), F32),
            pltpu.VMEM((2 * FREQS, SAMPLES), BF16),
            pltpu.VMEM((4, CH * PITCH, 128), F32),
            pltpu.VMEM((GROUPS, ROWS, CH), BF16),
            pltpu.SemaphoreType.DMA((2,)),
            pltpu.SemaphoreType.DMA((CH // CHUNK,)),
            pltpu.SemaphoreType.DMA((WIN // 2 // PART,)),
        ],
        compiler_params=pltpu.CompilerParams(vmem_limit_bytes=60 * 2**20),
        cost_estimate=pl.CostEstimate(flops=2 * 2**30, bytes_accessed=2**23, transcendentals=2**20),
        name="whiten",
    )(traces, jnp.asarray(taper_row()), jnp.asarray(forward_rows()))


def expand_kernel(spec, out, wide):
    lane = lax.broadcasted_iota(jnp.int32, (CH, ROWS), 1)
    for part in range(spec.shape[0]):
        turned = spec[part].astype(F32).T
        for f in range(4):
            kept = jnp.where(lane % 4 == f, turned, 0.0)
            for tile in range(2):
                wide[tile, pl.ds(f, CH, stride=4), :] = kept[:, tile * 128 : tile * 128 + 128]
        for tile in range(2):
            out[part, :, tile * 128 : tile * 128 + 128] = wide[tile].astype(BF16)


def expand(spec):
    per = 4
    return pl.pallas_call(
        expand_kernel,
        grid=(GROUPS // per,),
        out_shape=jax.ShapeDtypeStruct((GROUPS, 4 * CH, ROWS), BF16),
        in_specs=[pl.BlockSpec((per, ROWS, CH), lambda g: (g, 0, 0))],
        out_specs=pl.BlockSpec((per, 4 * CH, ROWS), lambda g: (g, 0, 0)),
        scratch_shapes=[pltpu.VMEM((2, 4 * CH, 128), F32)],
        compiler_params=pltpu.CompilerParams(vmem_limit_bytes=32 * 2**20),
        cost_estimate=pl.CostEstimate(flops=2**26, bytes_accessed=20 * 2**20, transcendentals=0),
        name="expand",
    )(spec)


def correlate_kernel(steps, own_hbm, partner_hbm, table, *refs):
    outs = refs[:4]
    own, partner, cross, own_sems, partner_sems = refs[4:]
    step = pl.program_id(0)
    per = GROUPS // steps
    sub = lax.broadcasted_iota(jnp.int32, (WIN, 8, CH), 1)

    def arrivals(chunk):
        groups = pl.ds(chunk * per, per)
        return (
            pltpu.make_async_copy(own_hbm.at[groups], own.at[groups], own_sems.at[chunk]),
            pltpu.make_async_copy(
                partner_hbm.at[groups], partner.at[groups], partner_sems.at[chunk]
            ),
        )

    @pl.when(step == 0)
    def _():
        for chunk in range(steps):
            for copy in arrivals(chunk):
                copy.start()

    @pl.when(step < steps)
    def _():
        for copy in arrivals(step):
            copy.wait()
        for pair in range(per // 2):
            halves = []
            for half in range(2):
                group = step * per + 2 * pair + half
                part = partner[group]
                wide = part.astype(F32).reshape(WIN, 8, CH)
                turned = jnp.where(sub < 4, -1.0, 1.0) * pltpu.roll(wide, 4, 1)
                right = jnp.concatenate([part, turned.reshape(ROWS, CH).astype(BF16)], axis=1)
                prod = jnp.dot(own[group], right, preferred_element_type=F32)
                halves.append(prod.reshape(CH // 2, 8, 2 * CH))
            rows = jnp.concatenate(halves, axis=1).astype(BF16)
            first = pl.multiple_of((step * (per // 2) + pair) * 16, 16)
            cross[:, pl.ds(first, 16), :] = rows

    @pl.when(step >= steps)
    def _():
        scale = 1.0 / math.sqrt(FREQS * WIN * N_TM)
        signs, chunk = outs[0].shape[1:3]
        base = (step - steps) * chunk

        def channel_pairs(idx, carry):
            first, second = cross[base + 2 * idx], cross[base + 2 * idx + 1]
            even = jnp.concatenate([first[:, :CH], second[:, :CH]], axis=1)
            odd = jnp.concatenate([first[:, CH:], second[:, CH:]], axis=1)
            even = jnp.dot(table[0], even, preferred_element_type=F32)
            odd = jnp.dot(table[1], odd, preferred_element_type=F32)
            for sign in range(signs):
                value = (even - odd if sign else even + odd) * scale
                value = value.astype(BF16).reshape(4, 2, 16, 2 * CH)
                for shift in range(4):
                    outs[shift][:, sign, 2 * idx] = value[shift, :, :, :CH]
                    outs[shift][:, sign, 2 * idx + 1] = value[shift, :, :, CH:]
            return carry

        lax.fori_loop(0, chunk // 2, channel_pairs, 0, unroll=8)


def correlate(own, partner, table, signs):
    per, chunk = 8, 16
    steps, late = GROUPS // per, CH // 2 // chunk
    block = pl.BlockSpec(
        (2, signs, chunk, 16, CH), lambda g: (0, 0, jnp.maximum(g - steps, 0), 0, 0)
    )
    return pl.pallas_call(
        functools.partial(correlate_kernel, steps),
        grid=(steps + late,),
        out_shape=[jax.ShapeDtypeStruct((2, signs, CH // 2, 16, CH), BF16)] * 4,
        in_specs=[
            pl.BlockSpec(memory_space=pl.ANY),
            pl.BlockSpec(memory_space=pl.ANY),
            pl.BlockSpec((2, 2 * LAGS, 2 * FREQS), lambda g: (0, 0, 0)),
        ],
        out_specs=[block] * 4,
        scratch_shapes=[
            pltpu.VMEM((GROUPS, 4 * CH, ROWS), BF16),
            pltpu.VMEM((GROUPS, ROWS, CH), BF16),
            pltpu.VMEM((CH // 2, 2 * FREQS, 2 * CH), BF16),
            pltpu.SemaphoreType.DMA((steps,)),
            pltpu.SemaphoreType.DMA((steps,)),
        ],
        compiler_params=pltpu.CompilerParams(vmem_limit_bytes=56 * 2**20),
        cost_estimate=pl.CostEstimate(flops=2**34, bytes_accessed=24 * 2**20, transcendentals=0),
        name="correlate_both" if signs == 2 else "correlate_one",
    )(own, partner, table)


def pick_kernel(index, source, out, held, in_sems, out_sems):
    blocks = range(held.shape[0])
    into = [
        pltpu.make_async_copy(source.at[index[c]], held.at[c], in_sems.at[c]) for c in blocks
    ]
    away = [pltpu.make_async_copy(held.at[c], out.at[c], out_sems.at[c]) for c in blocks]
    for copy in into:
        copy.start()
    for arrive, leave in zip(into, away):
        arrive.wait()
        leave.start()
    for copy in away:
        copy.wait()


def pick(source, index):
    return pl.pallas_call(
        pick_kernel,
        grid_spec=pltpu.PrefetchScalarGridSpec(
            num_scalar_prefetch=1,
            grid=(1,),
            in_specs=[pl.BlockSpec(memory_space=pltpu.HBM)],
            out_specs=pl.BlockSpec(memory_space=pltpu.HBM),
            scratch_shapes=[
                pltpu.VMEM(source.shape, source.dtype),
                pltpu.SemaphoreType.DMA((source.shape[0],)),
                pltpu.SemaphoreType.DMA((source.shape[0],)),
            ],
        ),
        out_shape=jax.ShapeDtypeStruct(source.shape, source.dtype),
        compiler_params=pltpu.CompilerParams(vmem_limit_bytes=58 * 2**20),
        cost_estimate=pl.CostEstimate(
            flops=0, bytes_accessed=2 * source.size * source.dtype.itemsize, transcendentals=0
        ),
        name="pick",
    )(index, source)


def at(values, index):
    hit = index[:, None] == jnp.arange(N_CHAN, dtype=jnp.int32)[None, :]
    return jnp.sum(jnp.where(hit, values[None, :], 0), axis=1)


def orient(pairing):
    zero, one = pairing[0], pairing[1]
    hop = at(one, zero)
    least = jnp.arange(N_CHAN, dtype=jnp.int32)
    for _ in range(3):
        least = jnp.minimum(least, at(least, hop))
        hop = at(hop, hop)
    handles_zero = least < at(least, zero)
    return handles_zero, jnp.where(handles_zero, zero, one), jnp.where(handles_zero, one, zero)


def over_chan(blocks):
    return lax.all_to_all(blocks, "chan", split_axis=0, concat_axis=0, tiled=True)


def sent_over_x(parts):
    got = [parts[0]]
    for shift in (1, 3, 2):
        route = [(x * 2 + y, (x + shift) % 4 * 2 + y) for x in range(4) for y in range(2)]
        got.append(lax.ppermute(parts[shift], "tm", route))
    return got


def sum_of(blocks):
    total = blocks[0].astype(F32)
    for block in blocks[1:]:
        total = total + block.astype(F32)
    return total


def sum_over_y(halves):
    mine = lax.axis_index("tm") % 2
    other = lax.dynamic_index_in_dim(halves, 1 - mine, 0, keepdims=False).astype(BF16)
    other = lax.ppermute(other, "tm", [(t, t ^ 1) for t in range(N_TM)])
    return lax.dynamic_index_in_dim(halves, mine, 0, keepdims=False) + other.astype(F32)


def body(traces, pairing):
    spec = whiten(traces)
    spread = over_chan(spec.reshape(N_CHAN, GROUPS // N_CHAN * ROWS, CH))
    own = expand(spec)
    handles_zero, handled, other = orient(pairing)
    table = jnp.asarray(np.concatenate([lag_rows()] * 2, axis=1))
    table = lax.dynamic_slice_in_dim(table, lax.axis_index("tm") // 2 * 32, 2 * LAGS, 1)
    spread, own, handled, other, table = lax.optimization_barrier(
        (spread, own, handled, other, table)
    )
    first = over_chan(pick(spread, handled)).reshape(GROUPS, ROWS, CH)
    second = over_chan(pick(spread, pairing[2])).reshape(GROUPS, ROWS, CH)
    pair_blocks = sent_over_x(correlate(own, first, table, 2))
    last_parts = correlate(own, second, table, 1)
    pair_blocks, last_parts = lax.optimization_barrier((pair_blocks, last_parts))
    pair_halves = sum_of(pair_blocks)
    last_blocks = sent_over_x(last_parts)
    behind = sum_over_y(pair_halves[:, 1])
    behind = over_chan(behind.reshape(N_CHAN, 64, CH).astype(BF16))
    behind = behind.at[other].get(mode="promise_in_bounds")
    last_blocks = lax.optimization_barrier((last_blocks, behind))[0]
    behind = over_chan(behind)
    ahead = sum_over_y(pair_halves[:, 0])
    last = sum_over_y(sum_of(last_blocks)[:, 0])

    def lags_first(value):
        return value.reshape(CH, 8, CH).transpose(1, 0, 2)

    forward = lags_first(ahead)
    backward = behind.astype(F32).reshape(CH, 8, CH).transpose(1, 2, 0)
    mine = lax.dynamic_index_in_dim(handles_zero, lax.axis_index("chan"), 0, keepdims=False)
    return jnp.stack(
        [
            jnp.where(mine, forward, backward),
            jnp.where(mine, backward, forward),
            lags_first(last),
        ]
    )


def solution(mesh):
    return jax.shard_map(
        body,
        mesh=mesh,
        in_specs=(P("chan", "tm", None), P()),
        out_specs=P(None, "tm", "chan", None),
        check_vma=False,
    )
```
